256 devices in a mesh: wide: 32 (over x, z_hi, core), narrow: 8 (over z_lo, y).
Axes of the slice: x: 4, y: 4, z: 8 (z_hi: 4, z_lo: 2; z = z_hi * 2 + z_lo), core: 2. Of those that a mesh axis runs over, the one named last changes fastest.
Arguments:
- acts: bfloat16 [4096, 4096], P('wide', 'narrow'), may hold values from -6 to 6
- grads: bfloat16 [4096, 14336], P('wide', 'narrow'), may hold values from -6 to 6
- basis_a: bfloat16 [4096, 4096], P(None, 'narrow'), may hold values from -4 to 4
- basis_g: bfloat16 [14336, 14336], P('narrow', 'wide'), may hold values from -4 to 4
- source_of_block: int32 [32, 1], replicated, may hold values from 0 to 15
- probe_blocks: int32 [1024, 2], replicated, may hold values from 0 to 31, all different within a row
Outputs:
- correction: float32 [4096, 14336], P('narrow', 'wide')
- influence: float32 [1024, 16], replicated
The draws below stay inside these ranges and needn't reach their ends.
Inputs may be any that keep to these rules, and one draw needn't show every extreme that they name: `probe_blocks`: each probe pair names two different blocks; every block is named by some pair. `source_of_block`: every source owns at least one block.
All inputs are finite; a program needn't handle non-finite values.
Results may differ from the reference program's by a relative error of at most 0.005.
Values may be sent and summed in bfloat16 or wider, within the bound.
A program may use at most 128 MiB of HBM per device.

```python
import math
import jax
import jax.numpy as jnp
from jax import lax

D = 4096
FF = 14336
BLOCK = 128
SOURCES = 16
PROBES = 1024
TOKENS = 4096
NB = 32


def column_scales(key, count, trend, spread):
    position = jnp.arange(count, dtype=jnp.float32) / max(count - 1, 1)
    wobble = jax.random.uniform(key, (count,), jnp.float32, -spread, spread)
    return jnp.power(trend, 0.5 * position) * jnp.power(10.0, wobble)


def basis_draw(key, count, trend, spread):
    key_entries, key_scale = jax.random.split(key)
    entries = jnp.clip(jax.random.normal(key_entries, (count, count), jnp.float32), -4.0, 4.0)
    scales = column_scales(key_scale, count, trend, spread)
    return (entries * scales[None, :] / math.sqrt(count)).astype(jnp.bfloat16)


def draw_basis_a(key, part):
    key = jax.random.fold_in(key, 11)
    return basis_draw(key, D, 3.0, 0.25)


def draw_basis_g(key, part):
    key = jax.random.fold_in(key, 23)
    return basis_draw(key, FF, 3.0, 0.25)


def block_levels(key, dims, cuts, low, largest):
    gain, own = 1.0, jax.random.fold_in(key, 6)
    for dim, blocks in cuts:
        steps = jnp.exp(jax.random.uniform(jax.random.fold_in(own, dim), (blocks,), jnp.float32, low / len(cuts), largest / len(cuts)))
        gain = gain * jnp.repeat(steps, dims[dim] // blocks).reshape([-1 if axis == dim else 1 for axis in range(len(dims))])
    return gain


def picks_of(stream_key, rows, count, top, lift):
    ranking = jax.random.permutation(jax.random.fold_in(stream_key, 1), count)
    boost = ranking
    for power in range(3):
        boost = boost * boost // count
    boost = boost * lift // count
    lots = jax.random.randint(jax.random.fold_in(stream_key, 2), (rows, count), 0, 4096) + boost
    holders = jax.random.permutation(jax.random.fold_in(stream_key, 3), rows)[jnp.arange(count) % rows]
    lots = jnp.where(jnp.arange(rows)[:, None] == holders[None, :], 1 << 14, lots)
    priority = lots * count + jnp.arange(count)
    return lax.top_k(priority.astype(jnp.int32), top)[1].astype(jnp.int32)


def centred(stream_key, extent, scale, bound, pieces=(), kind=jnp.bfloat16):
    values = scale * jax.random.normal(stream_key, extent, jnp.float32)
    if pieces:
        values = values * block_levels(stream_key, extent, pieces, -0.22, 0.18)
    return jnp.clip(values, -bound, bound).astype(kind)


def setup_inputs(seed: int = 0) -> dict:
    key_list = jax.random.split(jax.random.key(seed), 7)
    acts = centred(key_list[0], (TOKENS, D), 1.0, 6.0, ((0, 32), (1, 8)))
    grads = centred(key_list[1], (TOKENS, FF), 1.0, 6.0, ((0, 32), (1, 8)))
    basis_a = draw_basis_a(jax.random.fold_in(key_list[6], 71), 0)
    basis_g = draw_basis_g(jax.random.fold_in(key_list[6], 71), 0)
    source_of_block = picks_of(key_list[4], NB, SOURCES, 1, 0)
    probe_blocks = picks_of(key_list[5], PROBES, NB, 2, 0)
    return dict(acts=acts, grads=grads, basis_a=basis_a, basis_g=basis_g, source_of_block=source_of_block, probe_blocks=probe_blocks)


def reference(acts, grads, basis_a, basis_g, source_of_block, probe_blocks):
    rot_acts = jnp.dot(acts, basis_a, preferred_element_type=jnp.float32).astype(jnp.bfloat16)
    rot_grads = jnp.dot(grads, basis_g, preferred_element_type=jnp.float32).astype(jnp.bfloat16)
    sq_acts = jnp.square(rot_acts.astype(jnp.float32)).astype(jnp.bfloat16)
    sq_grads = jnp.square(rot_grads.astype(jnp.float32)).astype(jnp.bfloat16)
    correction = jnp.dot(sq_acts.T, sq_grads, preferred_element_type=jnp.float32) / TOKENS
    damping = 0.1 * jnp.mean(correction)
    denom = correction + damping
    blocks = TOKENS // BLOCK
    acts_blocks = rot_acts.astype(jnp.float32).reshape(blocks, BLOCK, D)
    grads_blocks = rot_grads.astype(jnp.float32).reshape(blocks, BLOCK, FF)
    width = min(128, D)

    def add_slice(step, kernel):
        first = (step * width).astype(jnp.int32)
        part_a = lax.dynamic_slice_in_dim(acts_blocks, first, width, 2)
        part_d = lax.dynamic_slice_in_dim(denom, first, width, 0)
        grad_tile = jnp.einsum('bti,btj->bij', part_a, grads_blocks)
        tile_back = lax.optimization_barrier(grad_tile.astype(jnp.bfloat16)).astype(jnp.float32)
        scaled = lax.optimization_barrier((tile_back / part_d[None]).astype(jnp.bfloat16)).astype(jnp.float32)
        return kernel + jnp.einsum('bij,cij->bc', tile_back, scaled)
    kernel = lax.fori_loop(0, D // width, add_slice, jnp.zeros((blocks, blocks), jnp.float32))
    ids = jnp.arange(blocks, dtype=jnp.int32)
    pick_c = (probe_blocks[:, 0:1] == ids[None, :]).astype(jnp.float32)
    pick_r = (probe_blocks[:, 1:2] == ids[None, :]).astype(jnp.float32)
    spread = jnp.dot(pick_c - pick_r, kernel, precision=lax.Precision.HIGHEST)
    keep = 1.0 - pick_c - pick_r
    owner = (source_of_block[:, 0:1] == jnp.arange(SOURCES, dtype=jnp.int32)[None, :]).astype(jnp.float32)
    factor = 1.0 / (BLOCK * math.sqrt(D * FF))
    influence = jnp.dot(spread * keep, owner, precision=lax.Precision.HIGHEST) * factor
    return (correction, influence)
```

```python
import functools
import math

import jax
import jax.numpy as jnp
from jax import lax
from jax.experimental import pallas as pl
from jax.experimental.pallas import tpu as pltpu
from jax.sharding import PartitionSpec as P

D = 4096
FF = 14336
BLOCK = 128
SOURCES = 16
NB = 32
TOKENS = 4096
ROWS = D // 8
COLS = FF // 32
MESH = pl.DeviceIdType.MESH
NT = (((1,), (1,)), ((), ()))
STAGES = (8, 8, 4)


def stage_peers():
    w, n = lax.axis_index("wide"), lax.axis_index("narrow")
    x, r = w // 8, w % 8

    def peer(stage, d):
        if stage == 0:
            return (w, (n + d) % 8)
        if stage == 1:
            return (x * 8 + (r + d) % 8, n)
        return (((x + d) % 4) * 8 + r, n)

    return peer, (n, r, x)


def sum_begin(stage, value, slots, send, recv):
    peer, mine = stage_peers()
    slots[mine[stage]] = value
    for d in range(1, STAGES[stage]):
        pltpu.make_async_remote_copy(
            src_ref=slots.at[mine[stage]],
            dst_ref=slots.at[mine[stage]],
            send_sem=send.at[d],
            recv_sem=recv.at[d],
            device_id=peer(stage, d),
            device_id_type=MESH,
        ).start()


def sum_end(stage, slots, send, recv):
    peer, mine = stage_peers()
    size = STAGES[stage]
    for d in range(1, size):
        source = (mine[stage] + size - d) % size
        copy = pltpu.make_async_remote_copy(
            src_ref=slots.at[mine[stage]],
            dst_ref=slots.at[source],
            send_sem=send.at[d],
            recv_sem=recv.at[d],
            device_id=peer(stage, d),
            device_id_type=MESH,
        )
        copy.wait()
    total = slots[0]
    for s in range(1, size):
        total = total + slots[s]
    return total


def influence_kernel(
    ra_ref, rg_ref, corr_ref, kern_ref, products, gram, recip, small, large, send_s, recv_s, send_l, recv_l
):
    peer, _ = stage_peers()
    barrier = pltpu.get_barrier_semaphore()
    count = 0
    for stage, size in enumerate(STAGES):
        for d in range(1, size):
            pl.semaphore_signal(barrier, inc=1, device_id=peer(stage, d), device_id_type=MESH)
            count += 1

    def square(value):
        value = value.astype(jnp.float32)
        return (value * value).astype(jnp.bfloat16)

    corr_ref[...] = jnp.zeros_like(corr_ref)

    def add_correction(step, carry):
        first = step * 4
        sa = jnp.concatenate([square(ra_ref[first + k]) for k in range(4)], axis=1)
        sg = jnp.concatenate([square(rg_ref[first + k]) for k in range(4)], axis=1)
        corr_ref[...] += lax.dot_general(sa, sg, NT, preferred_element_type=jnp.float32)
        return carry

    lax.fori_loop(0, NB // 4, add_correction, 0)
    corr_ref[...] = corr_ref[...] * (1.0 / TOKENS)
    total = jnp.full((8, 128), jnp.sum(corr_ref[...]), jnp.float32)
    pl.semaphore_wait(barrier, count)

    half = ROWS // 2

    def add_products(pair, carry):
        for part in range(2):
            tiles = []
            for k in range(2):
                tile = lax.dot_general(
                    ra_ref[2 * pair + k, pl.ds(part * half, half), :],
                    rg_ref[2 * pair + k],
                    NT,
                    preferred_element_type=jnp.float32,
                )
                tiles.append(tile.reshape(half // 8, 1, 8, COLS))
            both = jnp.concatenate(tiles, axis=1).reshape(half // 8, 16, COLS)
            products[pl.ds(part * (half // 8), half // 8), pl.ds(pl.multiple_of(pair * 16, 16), 16), :] = both.astype(
                jnp.bfloat16
            )
        return carry

    bounds = (0, 5, 10, 16)
    for stage in range(3):
        sum_begin(stage, total, small.at[stage], send_s.at[stage], recv_s.at[stage])
        lax.fori_loop(bounds[stage], bounds[stage + 1], add_products, 0)
        total = sum_end(stage, small.at[stage], send_s.at[stage], recv_s.at[stage])

    damping = (0.1 / (D * FF)) * total[0:1, 0:1]
    recip[...] = 1.0 / (corr_ref[...] + damping)
    gram[...] = jnp.zeros_like(gram)

    def add_gram(group, carry):
        tile = products[group]
        weights = recip[pl.ds(pl.multiple_of(group * 8, 8), 8), :]
        scaled = (tile.astype(jnp.float32).reshape(NB, 8, COLS) * weights[None]).astype(jnp.bfloat16)
        gram[...] += lax.dot_general(
            tile, scaled.reshape(NB * 8, COLS), NT, preferred_element_type=jnp.float32
        )
        return carry

    lax.fori_loop(0, ROWS // 8, add_gram, 0)
    width = NB * 8
    rows = lax.broadcasted_iota(jnp.int32, (width, width), 0) % 8
    cols = lax.broadcasted_iota(jnp.int32, (width, width), 1) % 8
    own = jnp.where(rows == cols, gram[...], 0.0).reshape(NB, 8, width)
    own = jnp.sum(own, axis=1)
    pick = lax.broadcasted_iota(jnp.int32, (width, 128), 0) // 8 == lax.broadcasted_iota(jnp.int32, (width, 128), 1)
    value = jnp.dot(
        own, pick.astype(jnp.float32), precision=lax.Precision.HIGHEST, preferred_element_type=jnp.float32
    )
    for stage in range(3):
        sum_begin(stage, value, large.at[stage], send_l.at[stage], recv_l.at[stage])
        value = sum_end(stage, large.at[stage], send_l.at[stage], recv_l.at[stage])
    kern_ref[...] = value


def influence_call(ra, rg):
    whole = pl.BlockSpec(memory_space=pltpu.VMEM)
    dma = pltpu.SemaphoreType.DMA
    return pl.pallas_call(
        influence_kernel,
        out_shape=(
            jax.ShapeDtypeStruct((ROWS, COLS), jnp.float32),
            jax.ShapeDtypeStruct((NB, 128), jnp.float32),
        ),
        in_specs=[whole, whole],
        out_specs=(whole, whole),
        scratch_shapes=[
            pltpu.VMEM((ROWS // 8, NB * 8, COLS), jnp.bfloat16),
            pltpu.VMEM((NB * 8, NB * 8), jnp.float32),
            pltpu.VMEM((ROWS, COLS), jnp.float32),
            pltpu.VMEM((3, 8, 8, 128), jnp.float32),
            pltpu.VMEM((3, 8, NB, 128), jnp.float32),
            dma((3, 8)),
            dma((3, 8)),
            dma((3, 8)),
            dma((3, 8)),
        ],
        compiler_params=pltpu.CompilerParams(
            collective_id=1, has_side_effects=True, vmem_limit_bytes=56 * 1024 * 1024
        ),
        cost_estimate=pl.CostEstimate(flops=10**10, bytes_accessed=10**7, transcendentals=0),
    )(ra, rg)


def on_device(acts, grads, basis_a, basis_g, source_of_block, probe_blocks):
    whole_acts = lax.all_gather(acts, "narrow", axis=1, tiled=True)
    rot_local = jnp.dot(whole_acts, basis_a, preferred_element_type=jnp.float32).astype(
        jnp.bfloat16
    )
    partial_sum = jnp.dot(
        lax.all_gather(grads, "wide", axis=0, tiled=True),
        basis_g,
        preferred_element_type=jnp.float32,
    )
    rot_acts = lax.all_gather(rot_local.T, "wide", axis=0, tiled=False)
    share = lax.psum_scatter(partial_sum, "narrow", scatter_dimension=0, tiled=True).astype(
        jnp.bfloat16
    )
    rot_grads = lax.all_gather(share, "narrow", axis=0, tiled=True)
    rot_grads = rot_grads.reshape(NB, BLOCK, COLS).transpose(0, 2, 1)
    correction, kernel = influence_call(rot_acts, rot_grads)
    kernel = kernel[:, :NB]
    block_ids = jnp.arange(NB, dtype=jnp.int32)
    pick_c = (probe_blocks[:, 0:1] == block_ids[None, :]).astype(jnp.float32)
    pick_r = (probe_blocks[:, 1:2] == block_ids[None, :]).astype(jnp.float32)
    spread = jnp.dot(pick_c - pick_r, kernel, precision=lax.Precision.HIGHEST)
    keep = 1.0 - pick_c - pick_r
    owner = (source_of_block == jnp.arange(SOURCES, dtype=jnp.int32)[None, :]).astype(jnp.float32)
    factor = 1.0 / (BLOCK * math.sqrt(D * FF))
    influence = jnp.dot(spread * keep, owner, precision=lax.Precision.HIGHEST) * factor
    return (correction, influence)


def solution(mesh):
    placed = (
        P("wide", "narrow"),
        P("wide", "narrow"),
        P(None, "narrow"),
        P("narrow", "wide"),
        P(),
        P(),
    )
    return jax.shard_map(
        on_device, mesh=mesh, in_specs=placed, out_specs=(P("narrow", "wide"), P()), check_vma=False
    )
```

```python
import functools
import math

import jax
import jax.numpy as jnp
from jax import lax
from jax.experimental import pallas as pl
from jax.experimental.pallas import tpu as pltpu
from jax.sharding import PartitionSpec as P

D = 4096
FF = 14336
BLOCK = 128
SOURCES = 16
NB = 32
TOKENS = 4096
ROWS = D // 8
COLS = FF // 32
MESH = pl.DeviceIdType.MESH
NT = (((1,), (1,)), ((), ()))
STAGES = (8, 8, 4)


def stage_peers():
    w, n = lax.axis_index("wide"), lax.axis_index("narrow")
    x, r = w // 8, w % 8

    def peer(stage, d):
        if stage == 0:
            return (w, (n + d) % 8)
        if stage == 1:
            return (x * 8 + (r + d) % 8, n)
        return (((x + d) % 4) * 8 + r, n)

    return peer, (n, r, x)


def sum_begin(stage, value, slots, send, recv):
    peer, mine = stage_peers()
    slots[mine[stage]] = value
    for d in range(1, STAGES[stage]):
        pltpu.make_async_remote_copy(
            src_ref=slots.at[mine[stage]],
            dst_ref=slots.at[mine[stage]],
            send_sem=send.at[d],
            recv_sem=recv.at[d],
            device_id=peer(stage, d),
            device_id_type=MESH,
        ).start()


def sum_end(stage, slots, send, recv):
    peer, mine = stage_peers()
    size = STAGES[stage]
    for d in range(1, size):
        source = (mine[stage] + size - d) % size
        copy = pltpu.make_async_remote_copy(
            src_ref=slots.at[mine[stage]],
            dst_ref=slots.at[source],
            send_sem=send.at[d],
            recv_sem=recv.at[d],
            device_id=peer(stage, d),
            device_id_type=MESH,
        )
        copy.wait()
    total = slots[0]
    for s in range(1, size):
        total = total + slots[s]
    return total


def influence_kernel(
    ra_ref, rg_ref, corr_ref, kern_ref, products, gram, recip, small, large, send_s, recv_s, send_l, recv_l
):
    peer, _ = stage_peers()
    barrier = pltpu.get_barrier_semaphore()
    count = 0
    for stage, size in enumerate(STAGES):
        for d in range(1, size):
            pl.semaphore_signal(barrier, inc=1, device_id=peer(stage, d), device_id_type=MESH)
            count += 1

    def square(value):
        value = value.astype(jnp.float32)
        return (value * value).astype(jnp.bfloat16)

    corr_ref[...] = jnp.zeros_like(corr_ref)

    def add_correction(step, carry):
        first = step * 4
        sa = jnp.concatenate([square(ra_ref[first + k]) for k in range(4)], axis=1)
        sg = jnp.concatenate([square(rg_ref[first + k]) for k in range(4)], axis=1)
        corr_ref[...] += lax.dot_general(sa, sg, NT, preferred_element_type=jnp.float32)
        return carry

    lax.fori_loop(0, NB // 4, add_correction, 0)
    corr_ref[...] = corr_ref[...] * (1.0 / TOKENS)
    total = jnp.full((8, 128), jnp.sum(corr_ref[...]), jnp.float32)
    pl.semaphore_wait(barrier, count)

    half = ROWS // 2

    def add_products(pair, carry):
        for part in range(2):
            tiles = []
            for k in range(2):
                tile = lax.dot_general(
                    ra_ref[2 * pair + k, pl.ds(part * half, half), :],
                    rg_ref[2 * pair + k],
                    NT,
                    preferred_element_type=jnp.float32,
                )
                tiles.append(tile.reshape(half // 8, 1, 8, COLS))
            both = jnp.concatenate(tiles, axis=1).reshape(half // 8, 16, COLS)
            products[pl.ds(part * (half // 8), half // 8), pl.ds(pl.multiple_of(pair * 16, 16), 16), :] = both.astype(
                jnp.bfloat16
            )
        return carry

    bounds = (0, 5, 10, 16)
    for stage in range(3):
        sum_begin(stage, total, small.at[stage], send_s.at[stage], recv_s.at[stage])
        lax.fori_loop(bounds[stage], bounds[stage + 1], add_products, 0)
        total = sum_end(stage, small.at[stage], send_s.at[stage], recv_s.at[stage])

    damping = (0.1 / (D * FF)) * total[0:1, 0:1]
    recip[...] = 1.0 / (corr_ref[...] + damping)
    gram[...] = jnp.zeros_like(gram)

    def add_gram(group, carry):
        tile = products[group]
        weights = recip[pl.ds(pl.multiple_of(group * 8, 8), 8), :]
        scaled = (tile.astype(jnp.float32).reshape(NB, 8, COLS) * weights[None]).astype(jnp.bfloat16)
        gram[...] += lax.dot_general(
            tile, scaled.reshape(NB * 8, COLS), NT, preferred_element_type=jnp.float32
        )
        return carry

    lax.fori_loop(0, ROWS // 8, add_gram, 0)
    width = NB * 8
    rows = lax.broadcasted_iota(jnp.int32, (width, width), 0) % 8
    cols = lax.broadcasted_iota(jnp.int32, (width, width), 1) % 8
    own = jnp.where(rows == cols, gram[...], 0.0).reshape(NB, 8, width)
    own = jnp.sum(own, axis=1)
    pick = lax.broadcasted_iota(jnp.int32, (width, 128), 0) // 8 == lax.broadcasted_iota(jnp.int32, (width, 128), 1)
    value = jnp.dot(
        own, pick.astype(jnp.float32), precision=lax.Precision.HIGHEST, preferred_element_type=jnp.float32
    )
    for stage in range(3):
        sum_begin(stage, value, large.at[stage], send_l.at[stage], recv_l.at[stage])
        value = sum_end(stage, large.at[stage], send_l.at[stage], recv_l.at[stage])
    kern_ref[...] = value


def influence_call(ra, rg):
    whole = pl.BlockSpec(memory_space=pltpu.VMEM)
    dma = pltpu.SemaphoreType.DMA
    return pl.pallas_call(
        influence_kernel,
        out_shape=(
            jax.ShapeDtypeStruct((ROWS, COLS), jnp.float32),
            jax.ShapeDtypeStruct((NB, 128), jnp.float32),
        ),
        in_specs=[whole, whole],
        out_specs=(whole, whole),
        scratch_shapes=[
            pltpu.VMEM((ROWS // 8, NB * 8, COLS), jnp.bfloat16),
            pltpu.VMEM((NB * 8, NB * 8), jnp.float32),
            pltpu.VMEM((ROWS, COLS), jnp.float32),
            pltpu.VMEM((3, 8, 8, 128), jnp.float32),
            pltpu.VMEM((3, 8, NB, 128), jnp.float32),
            dma((3, 8)),
            dma((3, 8)),
            dma((3, 8)),
            dma((3, 8)),
        ],
        compiler_params=pltpu.CompilerParams(
            collective_id=1, has_side_effects=True, vmem_limit_bytes=56 * 1024 * 1024
        ),
        cost_estimate=pl.CostEstimate(flops=10**10, bytes_accessed=10**7, transcendentals=0),
    )(ra, rg)


EVENTS = (
    (0, 0), (-1, 0), (1, 0), (0, -1), (0, 1), (2, 0), (0, 2), (-1, -1),
    (1, -1), (-1, 1), (1, 1), (2, -1), (2, 1), (-1, 2), (1, 2), (2, 2),
)
STEPS = len(EVENTS)
REDUCE_LAG = 4
FORWARD_LAG = 7


def table(step, values):
    picked = jnp.int32(values[0])
    for index, value in enumerate(values):
        if index:
            picked = jnp.where(step == index, jnp.int32(value), picked)
    return picked


class Place:
    def __init__(self):
        self.w, self.n = lax.axis_index("wide"), lax.axis_index("narrow")
        self.x, self.z, self.c = self.w // 8, (self.w // 2) % 4, self.w % 2

    def at(self, dx, dz, c):
        return ((self.x + dx + 4) % 4) * 8 + ((self.z + dz + 4) % 4) * 2 + c

    def owned(self, event, c):
        return self.at(*EVENTS[event], c)


class Relay:
    def __init__(self, place, buffer, send, recv, other):
        self.place, self.buffer, self.send, self.recv, self.other = place, buffer, send, recv, other
        self.half = buffer.shape[1] // 2

    def part(self, chunk, which):
        if which is None:
            return self.buffer.at[chunk]
        return self.buffer.at[chunk, pl.ds(which * self.half, self.half)]

    def copy(self, event, which, slot, recv_sem, dx, dz, dc=0):
        place = self.place
        ref = self.part(place.owned(event, place.c), which)
        c = (place.c + dc) % 2
        return pltpu.make_async_remote_copy(
            src_ref=ref,
            dst_ref=ref,
            send_sem=self.send.at[event, slot],
            recv_sem=recv_sem,
            device_id=(place.at(dx, dz, c), place.n),
            device_id_type=MESH,
        )

    def sends(self, event):
        dx, dz = EVENTS[event]
        recv = self.recv
        found = []
        if dx == 0:
            found.append(self.copy(event, None, 1, recv.at[EVENTS.index((-1, dz)), 0], 1, 0))
            found.append(self.copy(event, None, 2, recv.at[EVENTS.index((1, dz)), 0], -1, 0))
        if (dx, dz) == (0, 0):
            found.append(self.copy(event, None, 3, recv.at[EVENTS.index((0, -1)), 0], 0, 1))
            found.append(self.copy(event, None, 4, recv.at[EVENTS.index((0, 1)), 0], 0, -1))
        if (dx, dz) == (0, -1):
            found.append(self.copy(event, 0, 3, recv.at[EVENTS.index((0, 2)), 0], 0, 1))
        if (dx, dz) == (0, 1):
            found.append(self.copy(event, 1, 4, recv.at[EVENTS.index((0, 2)), 1], 0, -1))
        if dx == -1:
            found.append(self.copy(event, 0, 1, recv.at[EVENTS.index((2, dz)), 0], 1, 0))
        if dx == 1:
            found.append(self.copy(event, 1, 2, recv.at[EVENTS.index((2, dz)), 1], -1, 0))
        found.append(self.copy(event, None, 0, self.other.at[event], 0, 0, 1))
        return found

    def wait_arrival(self, event):
        dx, dz = EVENTS[event]
        if (dx, dz) == (0, 0):
            return
        halves = (0, 1) if dx == 2 or dz == 2 and dx == 0 else (None,)
        for which in halves:
            self.copy(event, which, 0, self.recv.at[event, which or 0], 0, 0, 1).wait_recv()

    def step(self, event):
        self.wait_arrival(event)
        for copy in self.sends(event):
            copy.start()

    def wait_other(self, event):
        place = self.place
        dx = table(event, [e[0] for e in EVENTS])
        dz = table(event, [e[1] for e in EVENTS])
        ref = self.buffer.at[place.at(dx, dz, 1 - place.c)]
        pltpu.make_async_remote_copy(
            src_ref=ref,
            dst_ref=ref,
            send_sem=self.send.at[0, 0],
            recv_sem=self.other.at[event],
            device_id=(place.at(0, 0, 1 - place.c), place.n),
            device_id_type=MESH,
        ).wait_recv()
        return place.at(dx, dz, 0)

    def finish(self):
        for event in range(STEPS):
            for copy in self.sends(event):
                copy.wait_send()


def rotate_kernel(
    acts_hbm, grads_hbm, basis_a_hbm, basis_g_hbm, ra, rg,
    grads, acts, basis_a, basis_g, basis_t, parts, shares,
    local, g_send, g_recv, g_other, r_send, r_recv, r_other,
    a_send, a_recv, s_send, s_recv, b_send, b_recv, f_send,
):
    place = Place()
    w, n, c = place.w, place.n, place.c
    width = acts_hbm.shape[1]
    own_cols = pl.ds(pl.multiple_of(n * width, width), width)
    fetch = [
        pltpu.make_async_copy(grads_hbm, grads.at[w], local.at[0]),
        pltpu.make_async_copy(acts_hbm, acts.at[:, own_cols], local.at[1]),
        pltpu.make_async_copy(basis_g_hbm, basis_g, local.at[2]),
        pltpu.make_async_copy(basis_a_hbm, basis_a, local.at[3]),
    ]
    for copy in fetch:
        copy.start()
    barrier = pltpu.get_barrier_semaphore()
    others = [(place.at(dx, dz, c), n) for dx, dz in ((1, 0), (-1, 0), (0, 1), (0, -1))]
    others += [(place.at(0, 0, 1 - c), n)] + [(w, (n + d) % 8) for d in range(1, 8)]
    for other in others:
        pl.semaphore_signal(barrier, inc=1, device_id=other, device_id_type=MESH)
    pl.semaphore_wait(barrier, len(others))

    g_relay = Relay(place, grads, g_send, g_recv, g_other)
    r_relay = Relay(place, ra, r_send, r_recv, r_other)
    fetch[0].wait()
    g_relay.step(0)

    def acts_copy(d):
        return pltpu.make_async_remote_copy(
            src_ref=acts.at[:, own_cols],
            dst_ref=acts.at[:, own_cols],
            send_sem=a_send.at[d],
            recv_sem=a_recv.at[d],
            device_id=(w, (n + d) % 8),
            device_id_type=MESH,
        )

    fetch[1].wait()
    for d in range(1, 8):
        acts_copy(d).start()
    fetch[2].wait()
    eye = (
        lax.broadcasted_iota(jnp.int32, (COLS, COLS), 0) == lax.broadcasted_iota(jnp.int32, (COLS, COLS), 1)
    ).astype(jnp.bfloat16)

    def turn(step, carry):
        span = pl.ds(pl.multiple_of(step * 256, 256), 256)
        basis_t[:, span] = lax.dot_general(
            eye, basis_g[span, :], NT, preferred_element_type=jnp.float32
        ).astype(jnp.bfloat16)
        return carry

    lax.fori_loop(0, basis_g.shape[0] // 256, turn, 0)
    fetch[3].wait()
    for d in range(1, 8):
        source = pl.ds(pl.multiple_of(((n + 8 - d) % 8) * width, width), width)
        pltpu.make_async_remote_copy(
            src_ref=acts.at[:, source],
            dst_ref=acts.at[:, source],
            send_sem=a_send.at[d],
            recv_sem=a_recv.at[d],
            device_id=(w, (n + d) % 8),
            device_id_type=MESH,
        ).wait_recv()
    turned = jnp.dot(acts[...], basis_a[...], preferred_element_type=jnp.float32)
    ra[w] = turned.T.astype(jnp.bfloat16)

    def share_copy(q, source, target):
        return pltpu.make_async_remote_copy(
            src_ref=parts.at[q],
            dst_ref=shares.at[q // 8, source],
            send_sem=s_send.at[q],
            recv_sem=s_recv.at[q // 8, source],
            device_id=(w, target),
            device_id_type=MESH,
        )

    def result_copy(block, q, send_sem, target):
        return pltpu.make_async_remote_copy(
            src_ref=rg.at[block],
            dst_ref=rg.at[block],
            send_sem=send_sem,
            recv_sem=b_recv.at[q],
            device_id=(w, target),
            device_id_type=MESH,
        )

    def line(d):
        return (n // 4) * 4 + (n + d) % 4

    def block_of(event, h):
        dx = table(event, [e[0] for e in EVENTS])
        dz = table(event, [e[1] for e in EVENTS])
        return place.at(dx, dz, h)

    def one_step(step, carry):
        for event in range(1, STEPS):
            pl.when(step == event)(functools.partial(g_relay.step, event))
        for event in range(STEPS):
            pl.when(step == (event + 4 if event else 2))(functools.partial(r_relay.step, event))

        @pl.when((step >= 1) & (step <= STEPS))
        def _():
            event = step - 1
            first = g_relay.wait_other(event)
            both = grads[pl.ds(first, 2)].reshape(2 * BLOCK, grads.shape[2])
            product = lax.dot_general(basis_t[...], both, NT, preferred_element_type=jnp.float32)
            for h in range(2):
                q = 2 * event + h
                parts[q] = product[:, h * BLOCK : (h + 1) * BLOCK].astype(jnp.bfloat16)

                @pl.when(q % 8 != n)
                def _():
                    share_copy(q, n, q % 8).start()

        @pl.when((step >= REDUCE_LAG) & (step < STEPS + REDUCE_LAG))
        def _():
            event = step - REDUCE_LAG
            for h in range(2):
                q = 2 * event + h

                @pl.when(q % 8 == n)
                def _():
                    total = parts[q].astype(jnp.float32)
                    for d in range(1, 8):
                        source = (n + d) % 8
                        share_copy(q, source, source).wait_recv()
                        total = total + shares[q // 8, source].astype(jnp.float32)
                    block = block_of(event, h)
                    rg[block] = total.astype(jnp.bfloat16)
                    result_copy(block, q, b_send.at[q // 8, 0], (n + 4) % 8).start()
                    for d in range(1, 4):
                        result_copy(block, q, b_send.at[q // 8, d], line(d)).start()

        @pl.when(step >= FORWARD_LAG)
        def _():
            event = step - FORWARD_LAG
            for h in range(2):
                q = 2 * event + h

                @pl.when(q % 8 == (n + 4) % 8)
                def _():
                    block = block_of(event, h)
                    result_copy(block, q, f_send.at[q // 8, 0], (n + 4) % 8).wait_recv()
                    for d in range(1, 4):
                        result_copy(block, q, f_send.at[q // 8, d], line(d)).start()

        return carry

    lax.fori_loop(1, STEPS + FORWARD_LAG, one_step, 0)
    for i in range(4):
        for d in range(1, 8):
            q = 8 * i + (n + d) % 8
            share_copy(q, n, (n + d) % 8).wait_send()
            if d != 4:
                result_copy(block_of(q // 2, q % 2), q, f_send.at[i, 0], (n + d) % 8).wait_recv()
        q = 8 * i + n
        block = block_of(q // 2, q % 2)
        result_copy(block, q, b_send.at[i, 0], (n + 4) % 8).wait_send()
        for d in range(1, 4):
            result_copy(block, q, b_send.at[i, d], line(d)).wait_send()
            result_copy(block, q, f_send.at[i, d], line(d)).wait_send()
    for event in range(STEPS):
        r_relay.wait_other(event)
    for d in range(1, 8):
        acts_copy(d).wait_send()
    g_relay.finish()
    r_relay.finish()


def rotate_call(acts, grads, basis_a, basis_g):
    anywhere = pl.BlockSpec(memory_space=pl.ANY)
    whole = pl.BlockSpec(memory_space=pltpu.VMEM)
    dma = pltpu.SemaphoreType.DMA
    bf16 = jnp.bfloat16
    hidden = grads.shape[1]
    return pl.pallas_call(
        rotate_kernel,
        out_shape=(
            jax.ShapeDtypeStruct((NB, ROWS, BLOCK), bf16),
            jax.ShapeDtypeStruct((NB, COLS, BLOCK), bf16),
        ),
        in_specs=[anywhere] * 4,
        out_specs=(whole, whole),
        scratch_shapes=[
            pltpu.VMEM((NB, BLOCK, hidden), bf16),
            pltpu.VMEM((BLOCK, D), bf16),
            pltpu.VMEM((D, ROWS), bf16),
            pltpu.VMEM((hidden, COLS), bf16),
            pltpu.VMEM((COLS, hidden), bf16),
            pltpu.VMEM((NB, COLS, BLOCK), bf16),
            pltpu.VMEM((4, 8, COLS, BLOCK), bf16),
            dma((4,)),
            dma((STEPS, 5)),
            dma((STEPS, 2)),
            dma((STEPS,)),
            dma((STEPS, 5)),
            dma((STEPS, 2)),
            dma((STEPS,)),
            dma((8,)),
            dma((8,)),
            dma((NB,)),
            dma((4, 8)),
            dma((4, 4)),
            dma((NB,)),
            dma((4, 4)),
        ],
        compiler_params=pltpu.CompilerParams(
            collective_id=2, has_side_effects=True, vmem_limit_bytes=56 * 1024 * 1024
        ),
        cost_estimate=pl.CostEstimate(flops=10**10, bytes_accessed=10**7, transcendentals=0),
    )(acts, grads, basis_a, basis_g)


def on_device(acts, grads, basis_a, basis_g, source_of_block, probe_blocks):
    rot_acts, rot_grads = rotate_call(acts, grads, basis_a, basis_g)
    correction, kernel = influence_call(rot_acts, rot_grads)
    kernel = kernel[:, :NB]
    block_ids = jnp.arange(NB, dtype=jnp.int32)
    pick_c = (probe_blocks[:, 0:1] == block_ids[None, :]).astype(jnp.float32)
    pick_r = (probe_blocks[:, 1:2] == block_ids[None, :]).astype(jnp.float32)
    spread = jnp.dot(pick_c - pick_r, kernel, precision=lax.Precision.HIGHEST)
    keep = 1.0 - pick_c - pick_r
    owner = (source_of_block == jnp.arange(SOURCES, dtype=jnp.int32)[None, :]).astype(jnp.float32)
    factor = 1.0 / (BLOCK * math.sqrt(D * FF))
    influence = jnp.dot(spread * keep, owner, precision=lax.Precision.HIGHEST) * factor
    return (correction, influence)


def solution(mesh):
    placed = (
        P("wide", "narrow"),
        P("wide", "narrow"),
        P(None, "narrow"),
        P("narrow", "wide"),
        P(),
        P(),
    )
    return jax.shard_map(
        on_device, mesh=mesh, in_specs=placed, out_specs=(P("narrow", "wide"), P()), check_vma=False
    )
```

```python
import functools
import math

import jax
import jax.numpy as jnp
from jax import lax
from jax.experimental import pallas as pl
from jax.experimental.pallas import tpu as pltpu
from jax.sharding import PartitionSpec as P

D = 4096
FF = 14336
BLOCK = 128
SOURCES = 16
NB = 32
TOKENS = 4096
ROWS = D // 8
COLS = FF // 32
MESH = pl.DeviceIdType.MESH
NT = (((1,), (1,)), ((), ()))
STAGES = (8, 8, 4)


def stage_peers():
    w, n = lax.axis_index("wide"), lax.axis_index("narrow")
    x, r = w // 8, w % 8

    def peer(stage, d):
        if stage == 0:
            return (w, (n + d) % 8)
        if stage == 1:
            return (x * 8 + (r + d) % 8, n)
        return (((x + d) % 4) * 8 + r, n)

    return peer, (n, r, x)


def sum_begin(stage, value, slots, send, recv):
    peer, mine = stage_peers()
    slots[mine[stage]] = value
    for d in range(1, STAGES[stage]):
        pltpu.make_async_remote_copy(
            src_ref=slots.at[mine[stage]],
            dst_ref=slots.at[mine[stage]],
            send_sem=send.at[d],
            recv_sem=recv.at[d],
            device_id=peer(stage, d),
            device_id_type=MESH,
        ).start()


def sum_end(stage, slots, send, recv):
    peer, mine = stage_peers()
    size = STAGES[stage]
    for d in range(1, size):
        source = (mine[stage] + size - d) % size
        copy = pltpu.make_async_remote_copy(
            src_ref=slots.at[mine[stage]],
            dst_ref=slots.at[source],
            send_sem=send.at[d],
            recv_sem=recv.at[d],
            device_id=peer(stage, d),
            device_id_type=MESH,
        )
        copy.wait()
    total = slots[0]
    for s in range(1, size):
        total = total + slots[s]
    return total


EVENTS = (
    (0, 0), (-1, 0), (1, 0), (0, -1), (0, 1), (2, 0), (0, 2), (-1, -1),
    (1, -1), (-1, 1), (1, 1), (2, -1), (2, 1), (-1, 2), (1, 2), (2, 2),
)
STEPS = len(EVENTS)
ACTS_STEP = 6
ACTS_LAG = 8
SUM_LAG = 3
RESULT_LAG = 5
PASS_LAG = 7
USE_LAG = 9
LATE = 6
HALF = COLS // 2
WIDE = 7


def table(step, values):
    picked = jnp.int32(values[0])
    for index, value in enumerate(values):
        if index:
            picked = jnp.where(step == index, jnp.int32(value), picked)
    return picked


class Place:
    def __init__(self):
        self.w, self.n = lax.axis_index("wide"), lax.axis_index("narrow")
        self.x, self.z, self.c = self.w // 8, (self.w // 2) % 4, self.w % 2

    def at(self, dx, dz, c):
        return ((self.x + dx + 4) % 4) * 8 + ((self.z + dz + 4) % 4) * 2 + c

    def owned(self, event, c):
        return self.at(*EVENTS[event], c)


class Relay:
    def __init__(self, place, buffer, send, recv, other):
        self.place, self.buffer, self.send, self.recv, self.other = place, buffer, send, recv, other
        self.half = buffer.shape[1] // 2

    def part(self, chunk, which):
        if which is None:
            return self.buffer.at[chunk]
        return self.buffer.at[chunk, pl.ds(which * self.half, self.half)]

    def copy(self, event, which, slot, recv_sem, dx, dz, dc=0):
        place = self.place
        ref = self.part(place.owned(event, place.c), which)
        c = (place.c + dc) % 2
        return pltpu.make_async_remote_copy(
            src_ref=ref,
            dst_ref=ref,
            send_sem=self.send.at[event, slot],
            recv_sem=recv_sem,
            device_id=(place.at(dx, dz, c), place.n),
            device_id_type=MESH,
        )

    def sends(self, event):
        dx, dz = EVENTS[event]
        recv = self.recv
        found = []
        if dx == 0:
            found.append(self.copy(event, None, 1, recv.at[EVENTS.index((-1, dz)), 0], 1, 0))
            found.append(self.copy(event, None, 2, recv.at[EVENTS.index((1, dz)), 0], -1, 0))
        if (dx, dz) == (0, 0):
            found.append(self.copy(event, None, 3, recv.at[EVENTS.index((0, -1)), 0], 0, 1))
            found.append(self.copy(event, None, 4, recv.at[EVENTS.index((0, 1)), 0], 0, -1))
        if (dx, dz) == (0, -1):
            found.append(self.copy(event, 0, 3, recv.at[EVENTS.index((0, 2)), 0], 0, 1))
        if (dx, dz) == (0, 1):
            found.append(self.copy(event, 1, 4, recv.at[EVENTS.index((0, 2)), 1], 0, -1))
        if dx == -1:
            found.append(self.copy(event, 0, 1, recv.at[EVENTS.index((2, dz)), 0], 1, 0))
        if dx == 1:
            found.append(self.copy(event, 1, 2, recv.at[EVENTS.index((2, dz)), 1], -1, 0))
        found.append(self.copy(event, None, 0, self.other.at[event], 0, 0, 1))
        return found

    def wait_arrival(self, event):
        dx, dz = EVENTS[event]
        if (dx, dz) == (0, 0):
            return
        halves = (0, 1) if dx == 2 or dz == 2 and dx == 0 else (None,)
        for which in halves:
            self.copy(event, which, 0, self.recv.at[event, which or 0], 0, 0, 1).wait_recv()

    def step(self, event):
        self.wait_arrival(event)
        for copy in self.sends(event):
            copy.start()

    def wait_other(self, event):
        place = self.place
        dx = table(event, [e[0] for e in EVENTS])
        dz = table(event, [e[1] for e in EVENTS])
        ref = self.buffer.at[place.at(dx, dz, 1 - place.c)]
        pltpu.make_async_remote_copy(
            src_ref=ref,
            dst_ref=ref,
            send_sem=self.send.at[0, 0],
            recv_sem=self.other.at[event],
            device_id=(place.at(0, 0, 1 - place.c), place.n),
            device_id_type=MESH,
        ).wait_recv()
        return place.at(dx, dz, 0)

    def finish(self):
        for event in range(STEPS):
            for copy in self.sends(event):
                copy.wait_send()


def whole_kernel(
    acts_hbm, grads_hbm, basis_a_hbm, basis_t_hbm, source_ref, probe_ref, corr, influence,
    grads, acts, basis_a, basis_t, parts, shares, crossed, ra, rg, products, gram, recip, small, large,
    local, g_send, g_recv, g_other, r_send, r_recv, r_other,
    a_send, a_recv, s_send, s_recv, z_send, z_recv, b_send, b_recv, f_send, send_s, recv_s, send_l, recv_l,
):
    place = Place()
    w, n, c = place.w, place.n, place.c
    y, line = n % 4, (n // 4) * 4
    width = acts_hbm.shape[1]
    own_cols = pl.ds(pl.multiple_of(n * width, width), width)
    fetch = [
        pltpu.make_async_copy(grads_hbm, grads.at[w], local.at[0]),
        pltpu.make_async_copy(acts_hbm, acts.at[:, own_cols], local.at[1]),
        pltpu.make_async_copy(basis_t_hbm, basis_t, local.at[2]),
        pltpu.make_async_copy(basis_a_hbm, basis_a, local.at[3]),
    ]
    for copy in fetch:
        copy.start()
    peer, _ = stage_peers()
    barrier = pltpu.get_barrier_semaphore()
    count = 0
    for stage, size in enumerate(STAGES):
        for d in range(1, size):
            pl.semaphore_signal(barrier, inc=1, device_id=peer(stage, d), device_id_type=MESH)
            count += 1
    pl.semaphore_wait(barrier, count)

    g_relay = Relay(place, grads, g_send, g_recv, g_other)
    r_relay = Relay(place, ra, r_send, r_recv, r_other)
    fetch[0].wait()
    g_relay.step(0)

    def acts_copy(d, source):
        cols = pl.ds(pl.multiple_of(source * width, width), width)
        return pltpu.make_async_remote_copy(
            src_ref=acts.at[:, cols],
            dst_ref=acts.at[:, cols],
            send_sem=a_send.at[d],
            recv_sem=a_recv.at[d],
            device_id=(w, (n + d) % 8),
            device_id_type=MESH,
        )

    fetch[1].wait()
    for d in range(1, 8):
        acts_copy(d, n).start()
    corr[...] = jnp.zeros_like(corr)
    gram[...] = jnp.zeros_like(gram)
    fetch[2].wait()

    def share_copy(q, source, target):
        return pltpu.make_async_remote_copy(
            src_ref=parts.at[q],
            dst_ref=shares.at[q // 4, source],
            send_sem=s_send.at[q],
            recv_sem=s_recv.at[q // 4, source],
            device_id=(w, line + target),
            device_id_type=MESH,
        )

    def cross_copy(q):
        return pltpu.make_async_remote_copy(
            src_ref=crossed.at[q // 4, 0],
            dst_ref=crossed.at[q // 4, 1],
            send_sem=z_send.at[q // 4],
            recv_sem=z_recv.at[q // 4],
            device_id=(w, (n + 4) % 8),
            device_id_type=MESH,
        )

    def result_copy(block, q, which, send_sem, d):
        ref = rg.at[block] if which is None else rg.at[block, pl.ds(which * HALF, HALF)]
        return pltpu.make_async_remote_copy(
            src_ref=ref,
            dst_ref=ref,
            send_sem=send_sem,
            recv_sem=b_recv.at[q, which or 0],
            device_id=(w, line + (y + d) % 4),
            device_id_type=MESH,
        )

    def first_of(event):
        return place.at(table(event, [e[0] for e in EVENTS]), table(event, [e[1] for e in EVENTS]), 0)

    def square(value):
        value = value.astype(jnp.float32)
        return (value * value).astype(jnp.bfloat16)

    def add_products(event, carry):
        first = first_of(event)
        tiles = []
        for k in range(2):
            tile = lax.dot_general(rg[first + k], ra[first + k], NT, preferred_element_type=jnp.float32)
            tiles.append(tile.reshape(COLS // (8 * WIDE), WIDE, 1, 8, ROWS))
        both = jnp.concatenate(tiles, axis=2).astype(jnp.bfloat16).reshape(COLS // (8 * WIDE), WIDE, 16, ROWS)
        for g in range(WIDE):
            products[:, pl.ds(pl.multiple_of(first * 8, 16), 16), g * ROWS : (g + 1) * ROWS] = both[:, g]
        return carry

    def one_step(step, carry):
        for event in range(1, STEPS):
            pl.when(step == event)(functools.partial(g_relay.step, event))

        @pl.when(step == ACTS_STEP)
        def _():
            fetch[3].wait()
            for d in range(1, 8):
                acts_copy(d, (n + 8 - d) % 8).wait_recv()
            turned = jnp.dot(acts[...], basis_a[...], preferred_element_type=jnp.float32)
            ra[w] = turned.T.astype(jnp.bfloat16)

        for event in range(STEPS):
            pl.when(step == (event + ACTS_LAG if event else ACTS_STEP))(functools.partial(r_relay.step, event))

        @pl.when((step >= 1) & (step <= STEPS))
        def _():
            event = step - 1
            first = g_relay.wait_other(event)
            both = grads[pl.ds(first, 2)].reshape(2 * BLOCK, grads.shape[2])
            product = lax.dot_general(basis_t[...], both, NT, preferred_element_type=jnp.float32)
            for h in range(2):
                q = 2 * event + h
                parts[q] = product[:, h * BLOCK : (h + 1) * BLOCK].astype(jnp.bfloat16)

                @pl.when(q % 4 != y)
                def _():
                    share_copy(q, y, q % 4).start()

        @pl.when((step >= SUM_LAG) & (step < STEPS + SUM_LAG))
        def _():
            event = step - SUM_LAG
            for h in range(2):
                q = 2 * event + h

                @pl.when(q % 4 == y)
                def _():
                    total = parts[q].astype(jnp.float32)
                    for d in range(1, 4):
                        source = (y + d) % 4
                        share_copy(q, source, source).wait_recv()
                        total = total + shares[q // 4, source].astype(jnp.float32)
                    crossed[q // 4, 0] = total.astype(jnp.bfloat16)
                    cross_copy(q).start()

        @pl.when((step >= RESULT_LAG) & (step < STEPS + RESULT_LAG))
        def _():
            event = step - RESULT_LAG
            for h in range(2):
                q = 2 * event + h

                @pl.when(q % 4 == y)
                def _():
                    cross_copy(q).wait_recv()
                    block = first_of(event) + h
                    total = crossed[q // 4, 0].astype(jnp.float32) + crossed[q // 4, 1].astype(jnp.float32)
                    rg[block] = total.astype(jnp.bfloat16)
                    result_copy(block, q, None, b_send.at[q // 4, 0], 1).start()
                    result_copy(block, q, None, b_send.at[q // 4, 1], 3).start()

        @pl.when((step >= PASS_LAG) & (step < STEPS + PASS_LAG))
        def _():
            event = step - PASS_LAG
            for h in range(2):
                q = 2 * event + h
                block = first_of(event) + h

                @pl.when(q % 4 == (y + 3) % 4)
                def _():
                    result_copy(block, q, None, f_send.at[q], 1).wait_recv()
                    result_copy(block, q, 0, f_send.at[q], 1).start()

                @pl.when(q % 4 == (y + 1) % 4)
                def _():
                    result_copy(block, q, None, f_send.at[q], 3).wait_recv()
                    result_copy(block, q, 1, f_send.at[q], 3).start()

        @pl.when(step >= USE_LAG)
        def _():
            event = step - USE_LAG
            first = first_of(event)
            for h in range(2):
                q = 2 * event + h

                @pl.when(q % 4 == (y + 2) % 4)
                def _():
                    for which in range(2):
                        result_copy(first + h, q, which, f_send.at[q], 1).wait_recv()

            r_relay.wait_other(event)
            sa = jnp.concatenate([square(ra[first + k]) for k in range(2)], axis=1)
            sg = jnp.concatenate([square(rg[first + k]) for k in range(2)], axis=1)
            corr[...] += lax.dot_general(sg, sa, NT, preferred_element_type=jnp.float32)

            @pl.when(event < STEPS - LATE)
            def _():
                add_products(event, 0)

        return carry

    lax.fori_loop(1, STEPS + USE_LAG, one_step, 0)
    moments = corr[...] * (1.0 / TOKENS)
    corr[...] = moments
    total = jnp.full((8, 128), jnp.sum(moments), jnp.float32)
    share = LATE // 3
    for stage in range(3):
        sum_begin(stage, total, small.at[stage], send_s.at[stage], recv_s.at[stage])
        first = STEPS - LATE + stage * share
        lax.fori_loop(first, first + share, add_products, 0)
        total = sum_end(stage, small.at[stage], send_s.at[stage], recv_s.at[stage])
    damping = (0.1 / (D * FF)) * total[0:1, 0:1]
    flipped = (1.0 / (corr[...] + damping)).reshape(COLS // (8 * WIDE), WIDE, 8, ROWS)
    for g in range(WIDE):
        recip[:, :, g * ROWS : (g + 1) * ROWS] = flipped[:, g]

    def add_gram(group, carry):
        tile = products[group]
        scaled = (tile.astype(jnp.float32).reshape(NB, 8, WIDE * ROWS) * recip[group][None]).astype(jnp.bfloat16)
        gram[...] += lax.dot_general(
            scaled.reshape(NB * 8, WIDE * ROWS), tile, NT, preferred_element_type=jnp.float32
        )
        return carry

    lax.fori_loop(0, COLS // (8 * WIDE), add_gram, 0)
    size = NB * 8
    rows = lax.broadcasted_iota(jnp.int32, (size, size), 0) % 8
    cols = lax.broadcasted_iota(jnp.int32, (size, size), 1) % 8
    own = jnp.where(rows == cols, gram[...], 0.0).reshape(NB, 8, size)
    own = jnp.sum(own, axis=1)
    pick = lax.broadcasted_iota(jnp.int32, (size, 128), 0) // 8 == lax.broadcasted_iota(jnp.int32, (size, 128), 1)
    exact = dict(precision=lax.Precision.HIGHEST, preferred_element_type=jnp.float32)
    kernel_t = jnp.dot(own, pick.astype(jnp.float32), **exact)
    for stage in range(3):
        sum_begin(stage, kernel_t, large.at[stage], send_l.at[stage], recv_l.at[stage])
        kernel_t = sum_end(stage, large.at[stage], send_l.at[stage], recv_l.at[stage])

    pairs = probe_ref.shape[1]
    ids = lax.broadcasted_iota(jnp.int32, (128, pairs), 0)
    pick_c = (probe_ref[0:1, :] == ids).astype(jnp.float32)
    pick_r = (probe_ref[1:2, :] == ids).astype(jnp.float32)
    spread = jnp.dot(kernel_t, pick_c - pick_r, **exact)
    keep = 1.0 - pick_c[:NB] - pick_r[:NB]
    owner = (source_ref[...] == lax.broadcasted_iota(jnp.int32, (SOURCES, NB), 0)).astype(jnp.float32)
    factor = 1.0 / (BLOCK * math.sqrt(D * FF))
    influence[...] = jnp.dot(owner, spread * keep, **exact) * factor

    for i in range(8):
        for d in range(1, 4):
            share_copy(4 * i + (y + d) % 4, y, (y + d) % 4).wait_send()
        cross_copy(4 * i).wait_send()
        result_copy(0, 0, None, b_send.at[i, 0], 1).wait_send()
        result_copy(0, 0, None, b_send.at[i, 1], 3).wait_send()
        result_copy(0, 0, 0, f_send.at[4 * i + (y + 3) % 4], 1).wait_send()
        result_copy(0, 0, 1, f_send.at[4 * i + (y + 1) % 4], 3).wait_send()
    for d in range(1, 8):
        acts_copy(d, n).wait_send()
    g_relay.finish()
    r_relay.finish()


def whole_call(acts, grads, basis_a, basis_t, source, probe):
    anywhere = pl.BlockSpec(memory_space=pl.ANY)
    whole = pl.BlockSpec(memory_space=pltpu.VMEM)
    dma = pltpu.SemaphoreType.DMA
    bf16, f32 = jnp.bfloat16, jnp.float32
    hidden = grads.shape[1]
    return pl.pallas_call(
        whole_kernel,
        out_shape=(
            jax.ShapeDtypeStruct((COLS, ROWS), f32),
            jax.ShapeDtypeStruct((SOURCES, probe.shape[1]), f32),
        ),
        in_specs=[anywhere] * 4 + [whole] * 2,
        out_specs=(whole, whole),
        scratch_shapes=[
            pltpu.VMEM((NB, BLOCK, hidden), bf16),
            pltpu.VMEM((BLOCK, D), bf16),
            pltpu.VMEM((D, ROWS), bf16),
            pltpu.VMEM((COLS, hidden), bf16),
            pltpu.VMEM((NB, COLS, BLOCK), bf16),
            pltpu.VMEM((8, 4, COLS, BLOCK), bf16),
            pltpu.VMEM((8, 2, COLS, BLOCK), bf16),
            pltpu.VMEM((NB, ROWS, BLOCK), bf16),
            pltpu.VMEM((NB, COLS, BLOCK), bf16),
            pltpu.VMEM((COLS // (8 * WIDE), NB * 8, WIDE * ROWS), bf16),
            pltpu.VMEM((NB * 8, NB * 8), f32),
            pltpu.VMEM((COLS // (8 * WIDE), 8, WIDE * ROWS), f32),
            pltpu.VMEM((3, 8, 8, 128), f32),
            pltpu.VMEM((3, 8, NB, 128), f32),
            dma((4,)),
            dma((STEPS, 5)),
            dma((STEPS, 2)),
            dma((STEPS,)),
            dma((STEPS, 5)),
            dma((STEPS, 2)),
            dma((STEPS,)),
            dma((8,)),
            dma((8,)),
            dma((NB,)),
            dma((8, 4)),
            dma((8,)),
            dma((8,)),
            dma((8, 2)),
            dma((NB, 2)),
            dma((NB,)),
            dma((3, 8)),
            dma((3, 8)),
            dma((3, 8)),
            dma((3, 8)),
        ],
        compiler_params=pltpu.CompilerParams(
            collective_id=1, has_side_effects=True, vmem_limit_bytes=60 * 1024 * 1024
        ),
        cost_estimate=pl.CostEstimate(flops=10**10, bytes_accessed=10**7, transcendentals=0),
    )(acts, grads, basis_a, basis_t, source, probe)


def on_device(acts, grads, basis_a, basis_g, source_of_block, probe_blocks):
    correction, influence = whole_call(
        acts, grads, basis_a, basis_g.T, source_of_block.T, probe_blocks.T
    )
    return (correction.T, influence.T)


def solution(mesh):
    placed = (
        P("wide", "narrow"),
        P("wide", "narrow"),
        P(None, "narrow"),
        P("narrow", "wide"),
        P(),
        P(),
    )
    return jax.shard_map(
        on_device, mesh=mesh, in_specs=placed, out_specs=(P("narrow", "wide"), P()), check_vma=False
    )
```

```python
import functools
import math

import jax
import jax.numpy as jnp
from jax import lax
from jax.experimental import pallas as pl
from jax.experimental.pallas import tpu as pltpu
from jax.sharding import PartitionSpec as P

D = 4096
FF = 14336
BLOCK = 128
SOURCES = 16
NB = 32
TOKENS = 4096
ROWS = D // 8
COLS = FF // 32
MESH = pl.DeviceIdType.MESH
NT = (((1,), (1,)), ((), ()))
STAGES = (16, 16)


def stage_peers():
    w, n = lax.axis_index("wide"), lax.axis_index("narrow")
    near, far = (w % 2) * 8 + n, w // 2

    def peer(stage, d):
        if stage == 0:
            other = (near + d) % 16
            return (far * 2 + other // 8, other % 8)
        return (((far + d) % 16) * 2 + w % 2, n)

    return peer, (near, far)


def sum_copy(stage, slots, send, recv, source, d):
    peer, _ = stage_peers()
    return pltpu.make_async_remote_copy(
        src_ref=slots.at[source],
        dst_ref=slots.at[source],
        send_sem=send,
        recv_sem=recv,
        device_id=peer(stage, d),
        device_id_type=MESH,
    )


def sum_begin(stage, value, slots, send, recv):
    mine = stage_peers()[1][stage]
    slots[mine] = value
    for d in range(1, STAGES[stage]):
        sum_copy(stage, slots, send, recv, mine, d).start()


def sum_end(stage, slots, send, recv):
    size = STAGES[stage]
    sum_copy(stage, slots, send, recv, pl.ds(0, size - 1), 1).wait()
    total = slots[0]
    for s in range(1, size):
        total = total + slots[s]
    return total


EVENTS = (
    (0, 0), (-1, 0), (1, 0), (0, -1), (0, 1), (2, 0), (0, 2), (-1, -1),
    (1, -1), (-1, 1), (1, 1), (2, -1), (2, 1), (-1, 2), (1, 2), (2, 2),
)
STEPS = len(EVENTS)
R_STEPS = (6,) + tuple(range(9, 24))
ORDER = 1
SUM_LAG = 3
RESULT_LAG = 5
PASS_LAG = 7
USE_LAG = 9
LATE = 6
HALF = COLS // 2
WIDE = 7


def table(step, values):
    picked = jnp.int32(values[0])
    for index, value in enumerate(values):
        if index:
            picked = jnp.where(step == index, jnp.int32(value), picked)
    return picked


class Place:
    def __init__(self):
        self.w, self.n = lax.axis_index("wide"), lax.axis_index("narrow")
        self.x, self.z, self.c = self.w // 8, (self.w // 2) % 4, self.w % 2

    def at(self, dx, dz, c):
        return ((self.x + dx + 4) % 4) * 8 + ((self.z + dz + 4) % 4) * 2 + c

    def owned(self, event, c):
        return self.at(*EVENTS[event], c)


class Relay:
    def __init__(self, place, buffer, send, recv, other):
        self.place, self.buffer, self.send, self.recv, self.other = place, buffer, send, recv, other
        self.half = buffer.shape[1] // 2

    def part(self, chunk, which):
        if which is None:
            return self.buffer.at[chunk]
        return self.buffer.at[chunk, pl.ds(which * self.half, self.half)]

    def copy(self, event, which, slot, recv_sem, dx, dz, dc=0):
        place = self.place
        ref = self.part(place.owned(event, place.c), which)
        c = (place.c + dc) % 2
        return pltpu.make_async_remote_copy(
            src_ref=ref,
            dst_ref=ref,
            send_sem=self.send.at[event, slot],
            recv_sem=recv_sem,
            device_id=(place.at(dx, dz, c), place.n),
            device_id_type=MESH,
        )

    def sends(self, event):
        dx, dz = EVENTS[event]
        recv = self.recv
        found = []
        if dx == 0:
            found.append(self.copy(event, None, 1, recv.at[EVENTS.index((-1, dz)), 0], 1, 0))
            found.append(self.copy(event, None, 2, recv.at[EVENTS.index((1, dz)), 0], -1, 0))
        if (dx, dz) == (0, 0):
            found.append(self.copy(event, None, 3, recv.at[EVENTS.index((0, -1)), 0], 0, 1))
            found.append(self.copy(event, None, 4, recv.at[EVENTS.index((0, 1)), 0], 0, -1))
        if (dx, dz) == (0, -1):
            found.append(self.copy(event, 0, 3, recv.at[EVENTS.index((0, 2)), 0], 0, 1))
        if (dx, dz) == (0, 1):
            found.append(self.copy(event, 1, 4, recv.at[EVENTS.index((0, 2)), 1], 0, -1))
        if dx == -1:
            found.append(self.copy(event, 0, 1, recv.at[EVENTS.index((2, dz)), 0], 1, 0))
        if dx == 1:
            found.append(self.copy(event, 1, 2, recv.at[EVENTS.index((2, dz)), 1], -1, 0))
        found.append(self.copy(event, None, 0, self.other.at[event], 0, 0, 1))
        return found

    def wait_arrival(self, event):
        dx, dz = EVENTS[event]
        if (dx, dz) == (0, 0):
            return
        halves = (0, 1) if dx == 2 or dz == 2 and dx == 0 else (None,)
        for which in halves:
            self.copy(event, which, 0, self.recv.at[event, which or 0], 0, 0, 1).wait_recv()

    def step(self, event):
        self.wait_arrival(event)
        for copy in self.sends(event):
            copy.start()

    def wait_other(self, event):
        place = self.place
        dx = table(event, [e[0] for e in EVENTS])
        dz = table(event, [e[1] for e in EVENTS])
        ref = self.buffer.at[place.at(dx, dz, 1 - place.c)]
        pltpu.make_async_remote_copy(
            src_ref=ref,
            dst_ref=ref,
            send_sem=self.send.at[0, 0],
            recv_sem=self.other.at[event],
            device_id=(place.at(0, 0, 1 - place.c), place.n),
            device_id_type=MESH,
        ).wait_recv()
        return place.at(dx, dz, 0)

    def finish(self):
        for event in range(STEPS):
            for copy in self.sends(event):
                copy.wait_send()


def whole_kernel(
    acts_hbm, grads_hbm, basis_a_hbm, basis_t_hbm, source_ref, probe_ref, corr, influence,
    grads, acts, basis_a, basis_t, parts, shares, crossed, ra, rg, products, gram, recip, small, large,
    local, g_send, g_recv, g_other, r_send, r_recv, r_other,
    a_send, a_recv, s_send, s_recv, z_send, z_recv, b_send, b_recv, f_send, send_s, recv_s, send_l, recv_l,
):
    place = Place()
    w, n, c = place.w, place.n, place.c
    y, line = n % 4, (n // 4) * 4
    width = acts_hbm.shape[1]
    own_cols = pl.ds(pl.multiple_of(n * width, width), width)
    fetch = [
        pltpu.make_async_copy(grads_hbm, grads.at[w], local.at[0]),
        pltpu.make_async_copy(acts_hbm, acts.at[:, own_cols], local.at[1]),
        pltpu.make_async_copy(basis_t_hbm, basis_t, local.at[2]),
        pltpu.make_async_copy(basis_a_hbm, basis_a, local.at[3]),
    ]
    for copy in fetch:
        copy.start()
    peer, _ = stage_peers()
    barrier = pltpu.get_barrier_semaphore()
    count = 0
    for stage, size in enumerate(STAGES):
        for d in range(1, size):
            pl.semaphore_signal(barrier, inc=1, device_id=peer(stage, d), device_id_type=MESH)
            count += 1
    pl.semaphore_wait(barrier, count)

    g_relay = Relay(place, grads, g_send, g_recv, g_other)
    r_relay = Relay(place, ra, r_send, r_recv, r_other)
    fetch[0].wait()
    g_relay.step(0)

    def acts_copy(d, source):
        cols = pl.ds(pl.multiple_of(source * width, width), width)
        return pltpu.make_async_remote_copy(
            src_ref=acts.at[:, cols],
            dst_ref=acts.at[:, cols],
            send_sem=a_send.at[d],
            recv_sem=a_recv.at[d],
            device_id=(w, (n + d) % 8),
            device_id_type=MESH,
        )

    fetch[1].wait()
    for d in range(1, 8):
        acts_copy(d, n).start()
    corr[...] = jnp.zeros_like(corr)
    gram[...] = jnp.zeros_like(gram)
    fetch[2].wait()

    def share_copy(q, source, target):
        return pltpu.make_async_remote_copy(
            src_ref=parts.at[q],
            dst_ref=shares.at[q // 4, source],
            send_sem=s_send.at[q],
            recv_sem=s_recv.at[q // 4, source],
            device_id=(w, line + target),
            device_id_type=MESH,
        )

    def cross_copy(q):
        return pltpu.make_async_remote_copy(
            src_ref=crossed.at[q // 4, 0],
            dst_ref=crossed.at[q // 4, 1],
            send_sem=z_send.at[q // 4],
            recv_sem=z_recv.at[q // 4],
            device_id=(w, (n + 4) % 8),
            device_id_type=MESH,
        )

    def result_copy(block, q, which, send_sem, d):
        ref = rg.at[block] if which is None else rg.at[block, pl.ds(which * HALF, HALF)]
        return pltpu.make_async_remote_copy(
            src_ref=ref,
            dst_ref=ref,
            send_sem=send_sem,
            recv_sem=b_recv.at[q, which or 0],
            device_id=(w, line + (y + d) % 4),
            device_id_type=MESH,
        )

    def first_of(event):
        return place.at(table(event, [e[0] for e in EVENTS]), table(event, [e[1] for e in EVENTS]), 0)

    def square(value):
        value = value.astype(jnp.float32)
        return (value * value).astype(jnp.bfloat16)

    def add_products(event, carry):
        first = first_of(event)
        tiles = []
        for k in range(2):
            tile = lax.dot_general(rg[first + k], ra[first + k], NT, preferred_element_type=jnp.float32)
            tiles.append(tile.reshape(COLS // (8 * WIDE), WIDE, 1, 8, ROWS))
        both = jnp.concatenate(tiles, axis=2).astype(jnp.bfloat16).reshape(COLS // (8 * WIDE), WIDE, 16, ROWS)
        for g in range(WIDE):
            products[:, pl.ds(pl.multiple_of(first * 8, 16), 16), g * ROWS : (g + 1) * ROWS] = both[:, g]
        return carry

    def one_step(step, carry):
        def relay():
            for event in range(1, STEPS):
                pl.when(step == event)(functools.partial(g_relay.step, event))

        if ORDER == 0:
            relay()

        @pl.when((step >= 1) & (step <= STEPS))
        def _():
            event = step - 1
            first = g_relay.wait_other(event)
            both = grads[pl.ds(first, 2)].reshape(2 * BLOCK, grads.shape[2])
            product = lax.dot_general(basis_t[...], both, NT, preferred_element_type=jnp.float32)
            for h in range(2):
                q = 2 * event + h
                parts[q] = product[:, h * BLOCK : (h + 1) * BLOCK].astype(jnp.bfloat16)

                @pl.when(q % 4 != y)
                def _():
                    share_copy(q, y, q % 4).start()

        if ORDER == 1:
            relay()

        @pl.when((step >= SUM_LAG) & (step < STEPS + SUM_LAG))
        def _():
            event = step - SUM_LAG
            for h in range(2):
                q = 2 * event + h

                @pl.when(q % 4 == y)
                def _():
                    total = parts[q].astype(jnp.float32)
                    for d in range(1, 4):
                        source = (y + d) % 4
                        share_copy(q, source, source).wait_recv()
                        total = total + shares[q // 4, source].astype(jnp.float32)
                    crossed[q // 4, 0] = total.astype(jnp.bfloat16)
                    cross_copy(q).start()

        @pl.when((step >= RESULT_LAG) & (step < STEPS + RESULT_LAG))
        def _():
            event = step - RESULT_LAG
            for h in range(2):
                q = 2 * event + h

                @pl.when(q % 4 == y)
                def _():
                    cross_copy(q).wait_recv()
                    block = first_of(event) + h
                    total = crossed[q // 4, 0].astype(jnp.float32) + crossed[q // 4, 1].astype(jnp.float32)
                    rg[block] = total.astype(jnp.bfloat16)
                    result_copy(block, q, None, b_send.at[q // 4, 0], 1).start()
                    result_copy(block, q, None, b_send.at[q // 4, 1], 3).start()

        @pl.when((step >= PASS_LAG) & (step < STEPS + PASS_LAG))
        def _():
            event = step - PASS_LAG
            for h in range(2):
                q = 2 * event + h
                block = first_of(event) + h

                @pl.when(q % 4 == (y + 3) % 4)
                def _():
                    result_copy(block, q, None, f_send.at[q], 1).wait_recv()
                    result_copy(block, q, 0, f_send.at[q], 1).start()

                @pl.when(q % 4 == (y + 1) % 4)
                def _():
                    result_copy(block, q, None, f_send.at[q], 3).wait_recv()
                    result_copy(block, q, 1, f_send.at[q], 3).start()

        @pl.when(step == R_STEPS[0])
        def _():
            fetch[3].wait()
            for d in range(1, 8):
                acts_copy(d, (n + 8 - d) % 8).wait_recv()
            turned = jnp.dot(acts[...], basis_a[...], preferred_element_type=jnp.float32)
            ra[w] = turned.T.astype(jnp.bfloat16)

        for event in range(STEPS):
            pl.when(step == (R_STEPS[event]))(functools.partial(r_relay.step, event))

        @pl.when(step >= USE_LAG)
        def _():
            event = step - USE_LAG
            first = first_of(event)
            for h in range(2):
                q = 2 * event + h

                @pl.when(q % 4 == (y + 2) % 4)
                def _():
                    for which in range(2):
                        result_copy(first + h, q, which, f_send.at[q], 1).wait_recv()

            r_relay.wait_other(event)
            sa = jnp.concatenate([square(ra[first + k]) for k in range(2)], axis=1)
            sg = jnp.concatenate([square(rg[first + k]) for k in range(2)], axis=1)
            corr[...] += lax.dot_general(sg, sa, NT, preferred_element_type=jnp.float32)

            @pl.when(event < STEPS - LATE)
            def _():
                add_products(event, 0)

        return carry

    lax.fori_loop(1, STEPS + USE_LAG, one_step, 0)
    moments = corr[...] * (1.0 / TOKENS)
    corr[...] = moments
    total = jnp.full((8, 128), jnp.sum(moments), jnp.float32)
    share = LATE // 2
    for stage in range(2):
        sum_begin(stage, total, small.at[stage], send_s.at[stage], recv_s.at[stage])
        first = STEPS - LATE + stage * share
        lax.fori_loop(first, first + share, add_products, 0)
        total = sum_end(stage, small.at[stage], send_s.at[stage], recv_s.at[stage])
    damping = (0.1 / (D * FF)) * total[0:1, 0:1]
    flipped = (1.0 / (corr[...] + damping)).reshape(COLS // (8 * WIDE), WIDE, 8, ROWS)
    for g in range(WIDE):
        recip[:, :, g * ROWS : (g + 1) * ROWS] = flipped[:, g]

    def add_gram(group, carry):
        tile = products[group]
        scaled = (tile.astype(jnp.float32).reshape(NB, 8, WIDE * ROWS) * recip[group][None]).astype(jnp.bfloat16)
        gram[...] += lax.dot_general(
            scaled.reshape(NB * 8, WIDE * ROWS), tile, NT, preferred_element_type=jnp.float32
        )
        return carry

    lax.fori_loop(0, COLS // (8 * WIDE), add_gram, 0)
    size = NB * 8
    rows = lax.broadcasted_iota(jnp.int32, (size, size), 0) % 8
    cols = lax.broadcasted_iota(jnp.int32, (size, size), 1) % 8
    own = jnp.where(rows == cols, gram[...], 0.0).reshape(NB, 8, size)
    own = jnp.sum(own, axis=1)
    pick = lax.broadcasted_iota(jnp.int32, (size, 128), 0) // 8 == lax.broadcasted_iota(jnp.int32, (size, 128), 1)
    exact = dict(precision=lax.Precision.HIGHEST, preferred_element_type=jnp.float32)
    kernel_t = jnp.dot(own, pick.astype(jnp.float32), **exact)
    packed = jnp.concatenate([kernel_t[8 * k : 8 * k + 8, :NB] for k in range(4)], axis=1)
    for stage in range(2):
        sum_begin(stage, packed, large.at[stage], send_l.at[stage], recv_l.at[stage])
        packed = sum_end(stage, large.at[stage], send_l.at[stage], recv_l.at[stage])
    kernel_t = jnp.concatenate([packed[:, NB * k : NB * k + NB] for k in range(4)], axis=0)

    pairs = probe_ref.shape[1]
    ids = lax.broadcasted_iota(jnp.int32, (NB, pairs), 0)
    pick_c = (probe_ref[0:1, :] == ids).astype(jnp.float32)
    pick_r = (probe_ref[1:2, :] == ids).astype(jnp.float32)
    spread = jnp.dot(kernel_t, pick_c - pick_r, **exact)
    keep = 1.0 - pick_c - pick_r
    owner = (source_ref[...] == lax.broadcasted_iota(jnp.int32, (SOURCES, NB), 0)).astype(jnp.float32)
    factor = 1.0 / (BLOCK * math.sqrt(D * FF))
    influence[...] = jnp.dot(owner, spread * keep, **exact) * factor

    for i in range(8):
        for d in range(1, 4):
            share_copy(4 * i + (y + d) % 4, y, (y + d) % 4).wait_send()
        cross_copy(4 * i).wait_send()
        result_copy(0, 0, None, b_send.at[i, 0], 1).wait_send()
        result_copy(0, 0, None, b_send.at[i, 1], 3).wait_send()
        result_copy(0, 0, 0, f_send.at[4 * i + (y + 3) % 4], 1).wait_send()
        result_copy(0, 0, 1, f_send.at[4 * i + (y + 1) % 4], 3).wait_send()
    for d in range(1, 8):
        acts_copy(d, n).wait_send()
    g_relay.finish()
    r_relay.finish()


def whole_call(acts, grads, basis_a, basis_t, source, probe):
    anywhere = pl.BlockSpec(memory_space=pl.ANY)
    whole = pl.BlockSpec(memory_space=pltpu.VMEM)
    dma = pltpu.SemaphoreType.DMA
    bf16, f32 = jnp.bfloat16, jnp.float32
    hidden = grads.shape[1]
    return pl.pallas_call(
        whole_kernel,
        out_shape=(
            jax.ShapeDtypeStruct((COLS, ROWS), f32),
            jax.ShapeDtypeStruct((SOURCES, probe.shape[1]), f32),
        ),
        in_specs=[anywhere] * 4 + [whole] * 2,
        out_specs=(whole, whole),
        scratch_shapes=[
            pltpu.VMEM((NB, BLOCK, hidden), bf16),
            pltpu.VMEM((BLOCK, D), bf16),
            pltpu.VMEM((D, ROWS), bf16),
            pltpu.VMEM((COLS, hidden), bf16),
            pltpu.VMEM((NB, COLS, BLOCK), bf16),
            pltpu.VMEM((8, 4, COLS, BLOCK), bf16),
            pltpu.VMEM((8, 2, COLS, BLOCK), bf16),
            pltpu.VMEM((NB, ROWS, BLOCK), bf16),
            pltpu.VMEM((NB, COLS, BLOCK), bf16),
            pltpu.VMEM((COLS // (8 * WIDE), NB * 8, WIDE * ROWS), bf16),
            pltpu.VMEM((NB * 8, NB * 8), f32),
            pltpu.VMEM((COLS // (8 * WIDE), 8, WIDE * ROWS), f32),
            pltpu.VMEM((2, 16, 8, 128), f32),
            pltpu.VMEM((2, 16, 8, 128), f32),
            dma((4,)),
            dma((STEPS, 5)),
            dma((STEPS, 2)),
            dma((STEPS,)),
            dma((STEPS, 5)),
            dma((STEPS, 2)),
            dma((STEPS,)),
            dma((8,)),
            dma((8,)),
            dma((NB,)),
            dma((8, 4)),
            dma((8,)),
            dma((8,)),
            dma((8, 2)),
            dma((NB, 2)),
            dma((NB,)),
            dma((2,)),
            dma((2,)),
            dma((2,)),
            dma((2,)),
        ],
        compiler_params=pltpu.CompilerParams(
            collective_id=1, has_side_effects=True, vmem_limit_bytes=60 * 1024 * 1024
        ),
        cost_estimate=pl.CostEstimate(flops=10**10, bytes_accessed=10**7, transcendentals=0),
    )(acts, grads, basis_a, basis_t, source, probe)


def on_device(acts, grads, basis_a, basis_g, source_of_block, probe_blocks):
    correction, influence = whole_call(
        acts, grads, basis_a, basis_g.T, source_of_block.T, probe_blocks.T
    )
    return (correction.T, influence.T)


def solution(mesh):
    placed = (
        P("wide", "narrow"),
        P("wide", "narrow"),
        P(None, "narrow"),
        P("narrow", "wide"),
        P(),
        P(),
    )
    return jax.shard_map(
        on_device, mesh=mesh, in_specs=placed, out_specs=(P("narrow", "wide"), P()), check_vma=False
    )
```

```python
import functools
import math

import jax
import jax.numpy as jnp
from jax import lax
from jax.experimental import pallas as pl
from jax.experimental.pallas import tpu as pltpu
from jax.sharding import PartitionSpec as P

D = 4096
FF = 14336
BLOCK = 128
SOURCES = 16
NB = 32
TOKENS = 4096
ROWS = D // 8
COLS = FF // 32
MESH = pl.DeviceIdType.MESH
NT = (((1,), (1,)), ((), ()))
STAGES = (16, 16)


def stage_peers():
    w, n = lax.axis_index("wide"), lax.axis_index("narrow")
    near, far = (w % 2) * 8 + n, w // 2

    def peer(stage, d):
        if stage == 0:
            other = (near + d) % 16
            return (far * 2 + other // 8, other % 8)
        return (((far + d) % 16) * 2 + w % 2, n)

    return peer, (near, far)


def sum_copy(stage, slots, send, recv, source, d):
    peer, _ = stage_peers()
    return pltpu.make_async_remote_copy(
        src_ref=slots.at[source],
        dst_ref=slots.at[source],
        send_sem=send,
        recv_sem=recv,
        device_id=peer(stage, d),
        device_id_type=MESH,
    )


def sum_begin(stage, value, slots, send, recv):
    mine = stage_peers()[1][stage]
    slots[mine] = value
    for d in range(1, STAGES[stage]):
        sum_copy(stage, slots, send, recv, mine, d).start()


def sum_end(stage, slots, send, recv):
    size = STAGES[stage]
    sum_copy(stage, slots, send, recv, pl.ds(0, size - 1), 1).wait()
    total = slots[0]
    for s in range(1, size):
        total = total + slots[s]
    return total


EVENTS = (
    (0, 0), (-1, 0), (1, 0), (0, -1), (0, 1), (2, 0), (0, 2), (-1, -1),
    (1, -1), (-1, 1), (1, 1), (2, -1), (2, 1), (-1, 2), (1, 2), (2, 2),
)
STEPS = len(EVENTS)
R_STEPS = (6,) + tuple(range(9, 24))
ORDER = 1
ENERGY_STEP = 8
SUM_LAG = 3
RESULT_LAG = 5
PASS_LAG = 7
USE_STEP = 17
HALF = COLS // 2
WIDE = 7


def table(step, values):
    picked = jnp.int32(values[0])
    for index, value in enumerate(values):
        if index:
            picked = jnp.where(step == index, jnp.int32(value), picked)
    return picked


class Place:
    def __init__(self):
        self.w, self.n = lax.axis_index("wide"), lax.axis_index("narrow")
        self.x, self.z, self.c = self.w // 8, (self.w // 2) % 4, self.w % 2

    def at(self, dx, dz, c):
        return ((self.x + dx + 4) % 4) * 8 + ((self.z + dz + 4) % 4) * 2 + c

    def owned(self, event, c):
        return self.at(*EVENTS[event], c)


class Relay:
    def __init__(self, place, buffer, send, recv, other):
        self.place, self.buffer, self.send, self.recv, self.other = place, buffer, send, recv, other
        self.half = buffer.shape[1] // 2

    def part(self, chunk, which):
        if which is None:
            return self.buffer.at[chunk]
        return self.buffer.at[chunk, pl.ds(which * self.half, self.half)]

    def copy(self, event, which, slot, recv_sem, dx, dz, dc=0):
        place = self.place
        ref = self.part(place.owned(event, place.c), which)
        c = (place.c + dc) % 2
        return pltpu.make_async_remote_copy(
            src_ref=ref,
            dst_ref=ref,
            send_sem=self.send.at[event, slot],
            recv_sem=recv_sem,
            device_id=(place.at(dx, dz, c), place.n),
            device_id_type=MESH,
        )

    def sends(self, event):
        dx, dz = EVENTS[event]
        recv = self.recv
        found = []
        if dx == 0:
            found.append(self.copy(event, None, 1, recv.at[EVENTS.index((-1, dz)), 0], 1, 0))
            found.append(self.copy(event, None, 2, recv.at[EVENTS.index((1, dz)), 0], -1, 0))
        if (dx, dz) == (0, 0):
            found.append(self.copy(event, None, 3, recv.at[EVENTS.index((0, -1)), 0], 0, 1))
            found.append(self.copy(event, None, 4, recv.at[EVENTS.index((0, 1)), 0], 0, -1))
        if (dx, dz) == (0, -1):
            found.append(self.copy(event, 0, 3, recv.at[EVENTS.index((0, 2)), 0], 0, 1))
        if (dx, dz) == (0, 1):
            found.append(self.copy(event, 1, 4, recv.at[EVENTS.index((0, 2)), 1], 0, -1))
        if dx == -1:
            found.append(self.copy(event, 0, 1, recv.at[EVENTS.index((2, dz)), 0], 1, 0))
        if dx == 1:
            found.append(self.copy(event, 1, 2, recv.at[EVENTS.index((2, dz)), 1], -1, 0))
        found.append(self.copy(event, None, 0, self.other.at[event], 0, 0, 1))
        return found

    def wait_arrival(self, event):
        dx, dz = EVENTS[event]
        if (dx, dz) == (0, 0):
            return
        halves = (0, 1) if dx == 2 or dz == 2 and dx == 0 else (None,)
        for which in halves:
            self.copy(event, which, 0, self.recv.at[event, which or 0], 0, 0, 1).wait_recv()

    def step(self, event):
        self.wait_arrival(event)
        for copy in self.sends(event):
            copy.start()

    def wait_other(self, event):
        place = self.place
        dx = table(event, [e[0] for e in EVENTS])
        dz = table(event, [e[1] for e in EVENTS])
        ref = self.buffer.at[place.at(dx, dz, 1 - place.c)]
        pltpu.make_async_remote_copy(
            src_ref=ref,
            dst_ref=ref,
            send_sem=self.send.at[0, 0],
            recv_sem=self.other.at[event],
            device_id=(place.at(0, 0, 1 - place.c), place.n),
            device_id_type=MESH,
        ).wait_recv()
        return place.at(dx, dz, 0)

    def finish(self):
        for event in range(STEPS):
            for copy in self.sends(event):
                copy.wait_send()


def whole_kernel(
    acts_hbm, grads_hbm, basis_a_hbm, basis_t_hbm, source_ref, probe_ref, corr, influence,
    grads, acts, basis_a, basis_t, parts, shares, crossed, ra, rg, products, gram, recip, small, large,
    energy, weight, weight_line, weight_own,
    local, g_send, g_recv, g_other, r_send, r_recv, r_other,
    a_send, a_recv, s_send, s_recv, z_send, z_recv, b_send, b_recv, f_send, send_s, recv_s, send_l, recv_l,
    l_send, l_recv, w_send, w_recv,
):
    place = Place()
    w, n, c = place.w, place.n, place.c
    y, line = n % 4, (n // 4) * 4
    width = acts_hbm.shape[1]
    own_cols = pl.ds(pl.multiple_of(n * width, width), width)
    fetch = [
        pltpu.make_async_copy(grads_hbm, grads.at[w], local.at[0]),
        pltpu.make_async_copy(acts_hbm, acts.at[:, own_cols], local.at[1]),
        pltpu.make_async_copy(basis_t_hbm, basis_t, local.at[2]),
        pltpu.make_async_copy(basis_a_hbm, basis_a, local.at[3]),
    ]
    for copy in fetch:
        copy.start()
    peer, _ = stage_peers()
    barrier = pltpu.get_barrier_semaphore()
    count = 0
    for stage, size in enumerate(STAGES):
        for d in range(1, size):
            pl.semaphore_signal(barrier, inc=1, device_id=peer(stage, d), device_id_type=MESH)
            count += 1
    for event in range(1, STEPS):
        dx, dz = EVENTS[event]
        pl.semaphore_signal(barrier, inc=1, device_id=(place.at(dx, dz, 1 - c), n), device_id_type=MESH)
        count += 1
    pl.semaphore_wait(barrier, count)

    g_relay = Relay(place, grads, g_send, g_recv, g_other)
    r_relay = Relay(place, ra, r_send, r_recv, r_other)
    fetch[0].wait()
    g_relay.step(0)

    def acts_copy(d, source):
        cols = pl.ds(pl.multiple_of(source * width, width), width)
        return pltpu.make_async_remote_copy(
            src_ref=acts.at[:, cols],
            dst_ref=acts.at[:, cols],
            send_sem=a_send.at[d],
            recv_sem=a_recv.at[d],
            device_id=(w, (n + d) % 8),
            device_id_type=MESH,
        )

    fetch[1].wait()
    for d in range(1, 8):
        acts_copy(d, n).start()
    corr[...] = jnp.zeros_like(corr)
    gram[...] = jnp.zeros_like(gram)
    fetch[2].wait()

    def share_copy(q, source, target):
        return pltpu.make_async_remote_copy(
            src_ref=parts.at[q],
            dst_ref=shares.at[q // 4, source],
            send_sem=s_send.at[q],
            recv_sem=s_recv.at[q // 4, source],
            device_id=(w, line + target),
            device_id_type=MESH,
        )

    def line_sum(q):
        total = parts[q].astype(jnp.float32)
        for d in range(1, 4):
            total = total + shares[q // 4, (y + d) % 4].astype(jnp.float32)
        return total

    def cross_copy(q):
        return pltpu.make_async_remote_copy(
            src_ref=crossed.at[q // 4, 0],
            dst_ref=crossed.at[q // 4, 1],
            send_sem=z_send.at[q // 4],
            recv_sem=z_recv.at[q // 4],
            device_id=(w, (n + 4) % 8),
            device_id_type=MESH,
        )

    def result_copy(block, q, which, send_sem, d):
        ref = rg.at[block] if which is None else rg.at[block, pl.ds(which * HALF, HALF)]
        return pltpu.make_async_remote_copy(
            src_ref=ref,
            dst_ref=ref,
            send_sem=send_sem,
            recv_sem=b_recv.at[q, which or 0],
            device_id=(w, line + (y + d) % 4),
            device_id_type=MESH,
        )

    def first_of(event):
        return place.at(table(event, [e[0] for e in EVENTS]), table(event, [e[1] for e in EVENTS]), 0)

    def square(value):
        value = value.astype(jnp.float32)
        return (value * value).astype(jnp.bfloat16)

    def add_products(event):
        first = first_of(event)
        tiles = []
        for k in range(2):
            tile = lax.dot_general(rg[first + k], ra[first + k], NT, preferred_element_type=jnp.float32)
            tiles.append(tile.reshape(COLS // (8 * WIDE), WIDE, 1, 8, ROWS))
        both = jnp.concatenate(tiles, axis=2).astype(jnp.bfloat16).reshape(COLS // (8 * WIDE), WIDE, 16, ROWS)
        for g in range(WIDE):
            products[:, pl.ds(pl.multiple_of(first * 8, 16), 16), g * ROWS : (g + 1) * ROWS] = both[:, g]

    def line_copy(source, d):
        return pltpu.make_async_remote_copy(
            src_ref=weight_line.at[source],
            dst_ref=weight_line.at[source],
            send_sem=l_send.at[d],
            recv_sem=l_recv.at[d],
            device_id=(w, line + (y + d) % 4),
            device_id_type=MESH,
        )

    def weight_copy(event, core):
        dx, dz = EVENTS[event]
        return pltpu.make_async_remote_copy(
            src_ref=weight_own,
            dst_ref=weight.at[event // 2],
            send_sem=w_send.at[event // 2, core],
            recv_sem=w_recv.at[event // 2],
            device_id=(place.at(-dx, -dz, core), n),
            device_id_type=MESH,
        )

    def hand_out(act):
        for event in range(STEPS):
            for core in range(2):
                gives = (y % 2 == c) & (y // 2 == event % 2)
                if event == 0:
                    gives = gives & (core != c)
                pl.when(gives)(functools.partial(act, event, core))

    def weight_slots(act):
        for slot in range(8):
            if slot == 0:
                pl.when((y // 2 == 1) | (y % 2 != c))(functools.partial(act, slot))
            else:
                act(slot)

    def use(event, carry):
        first = first_of(event)
        for h in range(2):
            q = 2 * event + h

            @pl.when(q % 4 == (y + 2) % 4)
            def _():
                for which in range(2):
                    result_copy(first + h, q, which, f_send.at[q], 1).wait_recv()

        r_relay.wait_other(event)
        sa = jnp.concatenate([square(ra[first + k]) for k in range(2)], axis=1)
        sg = jnp.concatenate([square(rg[first + k]) for k in range(2)], axis=1)
        corr[...] += lax.dot_general(sg, sa, NT, preferred_element_type=jnp.float32)

        add_products(event)
        return carry

    def one_step(step, carry):
        def relay():
            for event in range(1, STEPS):
                pl.when(step == event)(functools.partial(g_relay.step, event))

        if ORDER == 0:
            relay()

        @pl.when((step >= 1) & (step <= STEPS))
        def _():
            event = step - 1
            first = g_relay.wait_other(event)
            both = grads[pl.ds(first, 2)].reshape(2 * BLOCK, grads.shape[2])
            product = lax.dot_general(basis_t[...], both, NT, preferred_element_type=jnp.float32)
            for h in range(2):
                q = 2 * event + h
                parts[q] = product[:, h * BLOCK : (h + 1) * BLOCK].astype(jnp.bfloat16)

                @pl.when(q % 4 != y)
                def _():
                    share_copy(q, y, q % 4).start()

        if ORDER == 1:
            relay()

        @pl.when((step >= SUM_LAG) & (step < STEPS + SUM_LAG))
        def _():
            event = step - SUM_LAG
            for h in range(2):
                q = 2 * event + h

                @pl.when(q % 4 == y)
                def _():
                    for d in range(1, 4):
                        share_copy(q, (y + d) % 4, (y + d) % 4).wait_recv()
                    crossed[q // 4, 0] = line_sum(q).astype(jnp.bfloat16)
                    cross_copy(q).start()

        @pl.when((step >= RESULT_LAG) & (step < STEPS + RESULT_LAG))
        def _():
            event = step - RESULT_LAG
            for h in range(2):
                q = 2 * event + h

                @pl.when(q % 4 == y)
                def _():
                    cross_copy(q).wait_recv()
                    block = first_of(event) + h
                    total = (line_sum(q) + crossed[q // 4, 1].astype(jnp.float32)).astype(jnp.bfloat16)
                    rg[block] = total
                    energy[q // 4] = jnp.sum(square(total).astype(jnp.float32).reshape(COLS // 8, 8, BLOCK), axis=0)
                    result_copy(block, q, None, b_send.at[q // 4, 0], 1).start()
                    result_copy(block, q, None, b_send.at[q // 4, 1], 3).start()

        @pl.when((step >= PASS_LAG) & (step < STEPS + PASS_LAG))
        def _():
            event = step - PASS_LAG
            for h in range(2):
                q = 2 * event + h
                block = first_of(event) + h

                @pl.when(q % 4 == (y + 3) % 4)
                def _():
                    result_copy(block, q, None, f_send.at[q], 1).wait_recv()
                    result_copy(block, q, 0, f_send.at[q], 1).start()

                @pl.when(q % 4 == (y + 1) % 4)
                def _():
                    result_copy(block, q, None, f_send.at[q], 3).wait_recv()
                    result_copy(block, q, 1, f_send.at[q], 3).start()

        @pl.when(step == R_STEPS[0])
        def _():
            fetch[3].wait()
            for d in range(1, 8):
                acts_copy(d, (n + 8 - d) % 8).wait_recv()
            turned = jnp.dot(acts[...], basis_a[...], preferred_element_type=jnp.float32)
            own = turned.T.astype(jnp.bfloat16)
            ra[w] = own
            own = jnp.sum(square(own).astype(jnp.float32).reshape(ROWS // 8, 8, BLOCK), axis=0)
            weight_line[y] = jnp.broadcast_to(jnp.sum(own, axis=0, keepdims=True), (8, BLOCK))
            for d in range(1, 4):
                line_copy(y, d).start()

        for event in range(STEPS):
            pl.when(step == (R_STEPS[event]))(functools.partial(r_relay.step, event))

        @pl.when(step == ENERGY_STEP)
        def _():
            for d in range(1, 4):
                line_copy((y + 4 - d) % 4, d).wait_recv()
            weight_own[...] = weight_line[0] + weight_line[1] + weight_line[2] + weight_line[3]
            hand_out(lambda event, core: weight_copy(event, core).start())

            @pl.when((y // 2 == 0) & (y % 2 == c))
            def _():
                weight[0] = weight_own[...]

        @pl.when(step == STEPS + RESULT_LAG - 1)
        def _():
            weight_slots(lambda slot: weight_copy(2 * slot, 0).wait_recv())
            total = jnp.zeros((8, BLOCK), jnp.float32)
            for slot in range(8):
                total = total + weight[slot] * energy[slot]
            total = jnp.full((8, 128), jnp.sum(total), jnp.float32)
            sum_begin(0, total, small.at[0], send_s.at[0], recv_s.at[0])

        @pl.when(step == STEPS + RESULT_LAG + 1)
        def _():
            total = sum_end(0, small.at[0], send_s.at[0], recv_s.at[0])
            sum_begin(1, total, small.at[1], send_s.at[1], recv_s.at[1])

        @pl.when(step >= USE_STEP)
        def _():
            lax.fori_loop(2 * (step - USE_STEP), 2 * (step - USE_STEP) + 2, use, 0)

        return carry

    lax.fori_loop(1, USE_STEP + STEPS // 2, one_step, 0)
    moments = corr[...] * (1.0 / TOKENS)
    corr[...] = moments
    total = sum_end(1, small.at[1], send_s.at[1], recv_s.at[1])
    damping = (0.1 / (float(D) * FF * TOKENS)) * total[0:1, 0:1]
    flipped = (1.0 / (moments + damping)).reshape(COLS // (8 * WIDE), WIDE, 8, ROWS)
    for g in range(WIDE):
        recip[:, :, g * ROWS : (g + 1) * ROWS] = flipped[:, g]

    def add_gram(group, carry):
        tile = products[group]
        scaled = (tile.astype(jnp.float32).reshape(NB, 8, WIDE * ROWS) * recip[group][None]).astype(jnp.bfloat16)
        gram[...] += lax.dot_general(
            scaled.reshape(NB * 8, WIDE * ROWS), tile, NT, preferred_element_type=jnp.float32
        )
        return carry

    lax.fori_loop(0, COLS // (8 * WIDE), add_gram, 0)
    size = NB * 8
    rows = lax.broadcasted_iota(jnp.int32, (size, size), 0) % 8
    cols = lax.broadcasted_iota(jnp.int32, (size, size), 1) % 8
    own = jnp.where(rows == cols, gram[...], 0.0).reshape(NB, 8, size)
    own = jnp.sum(own, axis=1)
    pick = lax.broadcasted_iota(jnp.int32, (size, 128), 0) // 8 == lax.broadcasted_iota(jnp.int32, (size, 128), 1)
    exact = dict(precision=lax.Precision.HIGHEST, preferred_element_type=jnp.float32)
    kernel_t = jnp.dot(own, pick.astype(jnp.float32), **exact)
    packed = jnp.concatenate([kernel_t[8 * k : 8 * k + 8, :NB] for k in range(4)], axis=1)
    for stage in range(2):
        sum_begin(stage, packed, large.at[stage], send_l.at[stage], recv_l.at[stage])
        packed = sum_end(stage, large.at[stage], send_l.at[stage], recv_l.at[stage])
    kernel_t = jnp.concatenate([packed[:, NB * k : NB * k + NB] for k in range(4)], axis=0)

    pairs = probe_ref.shape[1]
    ids = lax.broadcasted_iota(jnp.int32, (NB, pairs), 0)
    pick_c = (probe_ref[0:1, :] == ids).astype(jnp.float32)
    pick_r = (probe_ref[1:2, :] == ids).astype(jnp.float32)
    spread = jnp.dot(kernel_t, pick_c - pick_r, **exact)
    keep = 1.0 - pick_c - pick_r
    owner = (source_ref[...] == lax.broadcasted_iota(jnp.int32, (SOURCES, NB), 0)).astype(jnp.float32)
    factor = 1.0 / (BLOCK * math.sqrt(D * FF))
    influence[...] = jnp.dot(owner, spread * keep, **exact) * factor

    for i in range(8):
        for d in range(1, 4):
            share_copy(4 * i + (y + d) % 4, y, (y + d) % 4).wait_send()
        cross_copy(4 * i).wait_send()
        result_copy(0, 0, None, b_send.at[i, 0], 1).wait_send()
        result_copy(0, 0, None, b_send.at[i, 1], 3).wait_send()
        result_copy(0, 0, 0, f_send.at[4 * i + (y + 3) % 4], 1).wait_send()
        result_copy(0, 0, 1, f_send.at[4 * i + (y + 1) % 4], 3).wait_send()
    for d in range(1, 8):
        acts_copy(d, n).wait_send()
    for d in range(1, 4):
        line_copy(y, d).wait_send()
    hand_out(lambda event, core: weight_copy(event, core).wait_send())
    g_relay.finish()
    r_relay.finish()


def whole_call(acts, grads, basis_a, basis_t, source, probe):
    anywhere = pl.BlockSpec(memory_space=pl.ANY)
    whole = pl.BlockSpec(memory_space=pltpu.VMEM)
    dma = pltpu.SemaphoreType.DMA
    bf16, f32 = jnp.bfloat16, jnp.float32
    hidden = grads.shape[1]
    return pl.pallas_call(
        whole_kernel,
        out_shape=(
            jax.ShapeDtypeStruct((COLS, ROWS), f32),
            jax.ShapeDtypeStruct((SOURCES, probe.shape[1]), f32),
        ),
        in_specs=[anywhere] * 4 + [whole] * 2,
        out_specs=(whole, whole),
        scratch_shapes=[
            pltpu.VMEM((NB, BLOCK, hidden), bf16),
            pltpu.VMEM((BLOCK, D), bf16),
            pltpu.VMEM((D, ROWS), bf16),
            pltpu.VMEM((COLS, hidden), bf16),
            pltpu.VMEM((NB, COLS, BLOCK), bf16),
            pltpu.VMEM((8, 4, COLS, BLOCK), bf16),
            pltpu.VMEM((8, 2, COLS, BLOCK), bf16),
            pltpu.VMEM((NB, ROWS, BLOCK), bf16),
            pltpu.VMEM((NB, COLS, BLOCK), bf16),
            pltpu.VMEM((COLS // (8 * WIDE), NB * 8, WIDE * ROWS), bf16),
            pltpu.VMEM((NB * 8, NB * 8), f32),
            pltpu.VMEM((COLS // (8 * WIDE), 8, WIDE * ROWS), f32),
            pltpu.VMEM((2, 16, 8, 128), f32),
            pltpu.VMEM((2, 16, 8, 128), f32),
            pltpu.VMEM((8, 8, 128), f32),
            pltpu.VMEM((8, 8, 128), f32),
            pltpu.VMEM((4, 8, 128), f32),
            pltpu.VMEM((8, 128), f32),
            dma((4,)),
            dma((STEPS, 5)),
            dma((STEPS, 2)),
            dma((STEPS,)),
            dma((STEPS, 5)),
            dma((STEPS, 2)),
            dma((STEPS,)),
            dma((8,)),
            dma((8,)),
            dma((NB,)),
            dma((8, 4)),
            dma((8,)),
            dma((8,)),
            dma((8, 2)),
            dma((NB, 2)),
            dma((NB,)),
            dma((2,)),
            dma((2,)),
            dma((2,)),
            dma((2,)),
            dma((4,)),
            dma((4,)),
            dma((8, 2)),
            dma((8,)),
        ],
        compiler_params=pltpu.CompilerParams(
            collective_id=1, has_side_effects=True, vmem_limit_bytes=60 * 1024 * 1024
        ),
        cost_estimate=pl.CostEstimate(flops=10**10, bytes_accessed=10**7, transcendentals=0),
    )(acts, grads, basis_a, basis_t, source, probe)


def on_device(acts, grads, basis_a, basis_g, source_of_block, probe_blocks):
    correction, influence = whole_call(
        acts, grads, basis_a, basis_g.T, source_of_block.T, probe_blocks.T
    )
    return (correction.T, influence.T)


def solution(mesh):
    placed = (
        P("wide", "narrow"),
        P("wide", "narrow"),
        P(None, "narrow"),
        P("narrow", "wide"),
        P(),
        P(),
    )
    return jax.shard_map(
        on_device, mesh=mesh, in_specs=placed, out_specs=(P("narrow", "wide"), P()), check_vma=False
    )
```

```python
import functools
import math

import jax
import jax.numpy as jnp
from jax import lax
from jax.experimental import pallas as pl
from jax.experimental.pallas import tpu as pltpu
from jax.sharding import PartitionSpec as P

D = 4096
FF = 14336
BLOCK = 128
SOURCES = 16
NB = 32
TOKENS = 4096
ROWS = D // 8
COLS = FF // 32
MESH = pl.DeviceIdType.MESH
NT = (((1,), (1,)), ((), ()))
STAGES = (16, 16)


def stage_peers():
    w, n = lax.axis_index("wide"), lax.axis_index("narrow")
    near, far = (w % 2) * 8 + n, w // 2

    def peer(stage, d):
        if stage == 0:
            other = (near + d) % 16
            return (far * 2 + other // 8, other % 8)
        return (((far + d) % 16) * 2 + w % 2, n)

    return peer, (near, far)


def sum_copy(stage, slots, send, recv, source, d):
    peer, _ = stage_peers()
    return pltpu.make_async_remote_copy(
        src_ref=slots.at[source],
        dst_ref=slots.at[source],
        send_sem=send,
        recv_sem=recv,
        device_id=peer(stage, d),
        device_id_type=MESH,
    )


def sum_begin(stage, value, slots, send, recv):
    mine = stage_peers()[1][stage]
    slots[mine] = value
    for d in range(1, STAGES[stage]):
        sum_copy(stage, slots, send, recv, mine, d).start()


def sum_end(stage, slots, send, recv):
    size = STAGES[stage]
    sum_copy(stage, slots, send, recv, pl.ds(0, size - 1), 1).wait()
    total = slots[0]
    for s in range(1, size):
        total = total + slots[s]
    return total


EVENTS = (
    (0, 0), (-1, 0), (1, 0), (0, -1), (0, 1), (2, 0), (0, 2), (-1, -1),
    (1, -1), (-1, 1), (1, 1), (2, -1), (2, 1), (-1, 2), (1, 2), (2, 2),
)
STEPS = len(EVENTS)
R_STEPS = (6,) + tuple(range(9, 24))
ORDER = 1
ENERGY_STEP = 8
SUM_LAG = 3
RESULT_LAG = 6
PASS_LAG = 8
USE_STEP = 17
HALF = COLS // 2
WIDE = 7


def table(step, values):
    picked = jnp.int32(values[0])
    for index, value in enumerate(values):
        if index:
            picked = jnp.where(step == index, jnp.int32(value), picked)
    return picked


class Place:
    def __init__(self):
        self.w, self.n = lax.axis_index("wide"), lax.axis_index("narrow")
        self.x, self.z, self.c = self.w // 8, (self.w // 2) % 4, self.w % 2

    def at(self, dx, dz, c):
        return ((self.x + dx + 4) % 4) * 8 + ((self.z + dz + 4) % 4) * 2 + c

    def owned(self, event, c):
        return self.at(*EVENTS[event], c)


class Relay:
    def __init__(self, place, buffer, send, recv, other):
        self.place, self.buffer, self.send, self.recv, self.other = place, buffer, send, recv, other
        self.half = buffer.shape[1] // 2

    def part(self, chunk, which):
        if which is None:
            return self.buffer.at[chunk]
        return self.buffer.at[chunk, pl.ds(which * self.half, self.half)]

    def copy(self, event, which, slot, recv_sem, dx, dz, dc=0):
        place = self.place
        ref = self.part(place.owned(event, place.c), which)
        c = (place.c + dc) % 2
        return pltpu.make_async_remote_copy(
            src_ref=ref,
            dst_ref=ref,
            send_sem=self.send.at[event, slot],
            recv_sem=recv_sem,
            device_id=(place.at(dx, dz, c), place.n),
            device_id_type=MESH,
        )

    def sends(self, event):
        dx, dz = EVENTS[event]
        recv = self.recv
        found = []
        if dx == 0:
            found.append(self.copy(event, None, 1, recv.at[EVENTS.index((-1, dz)), 0], 1, 0))
            found.append(self.copy(event, None, 2, recv.at[EVENTS.index((1, dz)), 0], -1, 0))
        if (dx, dz) == (0, 0):
            found.append(self.copy(event, None, 3, recv.at[EVENTS.index((0, -1)), 0], 0, 1))
            found.append(self.copy(event, None, 4, recv.at[EVENTS.index((0, 1)), 0], 0, -1))
        if (dx, dz) == (0, -1):
            found.append(self.copy(event, 0, 3, recv.at[EVENTS.index((0, 2)), 0], 0, 1))
        if (dx, dz) == (0, 1):
            found.append(self.copy(event, 1, 4, recv.at[EVENTS.index((0, 2)), 1], 0, -1))
        if dx == -1:
            found.append(self.copy(event, 0, 1, recv.at[EVENTS.index((2, dz)), 0], 1, 0))
        if dx == 1:
            found.append(self.copy(event, 1, 2, recv.at[EVENTS.index((2, dz)), 1], -1, 0))
        found.append(self.copy(event, None, 0, self.other.at[event], 0, 0, 1))
        return found

    def wait_arrival(self, event):
        dx, dz = EVENTS[event]
        if (dx, dz) == (0, 0):
            return
        halves = (0, 1) if dx == 2 or dz == 2 and dx == 0 else (None,)
        for which in halves:
            self.copy(event, which, 0, self.recv.at[event, which or 0], 0, 0, 1).wait_recv()

    def step(self, event):
        self.wait_arrival(event)
        for copy in self.sends(event):
            copy.start()

    def wait_other(self, event):
        place = self.place
        dx = table(event, [e[0] for e in EVENTS])
        dz = table(event, [e[1] for e in EVENTS])
        ref = self.buffer.at[place.at(dx, dz, 1 - place.c)]
        pltpu.make_async_remote_copy(
            src_ref=ref,
            dst_ref=ref,
            send_sem=self.send.at[0, 0],
            recv_sem=self.other.at[event],
            device_id=(place.at(0, 0, 1 - place.c), place.n),
            device_id_type=MESH,
        ).wait_recv()
        return place.at(dx, dz, 0)

    def finish(self):
        for event in range(STEPS):
            for copy in self.sends(event):
                copy.wait_send()


def whole_kernel(
    acts_hbm, grads_hbm, basis_a_hbm, basis_t_hbm, source_ref, probe_ref, corr, influence,
    grads, acts, basis_a, basis_t, parts, shares, crossed, ra, rg, products, gram, recip, small, large,
    energy, weight, weight_line, weight_own,
    local, g_send, g_recv, g_other, r_send, r_recv, r_other,
    a_send, a_recv, s_send, s_recv, z_send, z_recv, b_send, b_recv, f_send, send_s, recv_s, send_l, recv_l,
    l_send, l_recv, w_send, w_recv,
):
    place = Place()
    w, n, c = place.w, place.n, place.c
    y, line = n % 4, (n // 4) * 4
    width = acts_hbm.shape[1]
    own_cols = pl.ds(pl.multiple_of(n * width, width), width)
    fetch = [
        pltpu.make_async_copy(grads_hbm, grads.at[w], local.at[0]),
        pltpu.make_async_copy(acts_hbm, acts.at[:, own_cols], local.at[1]),
        pltpu.make_async_copy(basis_t_hbm, basis_t, local.at[2]),
        pltpu.make_async_copy(basis_a_hbm, basis_a, local.at[3]),
    ]
    for copy in fetch:
        copy.start()
    peer, _ = stage_peers()
    barrier = pltpu.get_barrier_semaphore()
    count = 0
    for stage, size in enumerate(STAGES):
        for d in range(1, size):
            pl.semaphore_signal(barrier, inc=1, device_id=peer(stage, d), device_id_type=MESH)
            count += 1
    for event in range(1, STEPS):
        dx, dz = EVENTS[event]
        pl.semaphore_signal(barrier, inc=1, device_id=(place.at(dx, dz, 1 - c), n), device_id_type=MESH)
        count += 1
    pl.semaphore_wait(barrier, count)

    g_relay = Relay(place, grads, g_send, g_recv, g_other)
    r_relay = Relay(place, ra, r_send, r_recv, r_other)
    fetch[0].wait()
    g_relay.step(0)

    def acts_copy(d, source):
        cols = pl.ds(pl.multiple_of(source * width, width), width)
        return pltpu.make_async_remote_copy(
            src_ref=acts.at[:, cols],
            dst_ref=acts.at[:, cols],
            send_sem=a_send.at[d],
            recv_sem=a_recv.at[d],
            device_id=(w, (n + d) % 8),
            device_id_type=MESH,
        )

    fetch[1].wait()
    for d in range(1, 8):
        acts_copy(d, n).start()
    corr[...] = jnp.zeros_like(corr)
    gram[...] = jnp.zeros_like(gram)
    fetch[2].wait()

    def share_copy(q, source, target):
        return pltpu.make_async_remote_copy(
            src_ref=parts.at[q],
            dst_ref=shares.at[q // 4, source],
            send_sem=s_send.at[q],
            recv_sem=s_recv.at[q // 4, source],
            device_id=(w, line + target),
            device_id_type=MESH,
        )

    def line_sum(q):
        total = parts[q].astype(jnp.float32)
        for d in range(1, 4):
            total = total + shares[q // 4, (y + d) % 4].astype(jnp.float32)
        return total

    def cross_copy(q):
        return pltpu.make_async_remote_copy(
            src_ref=crossed.at[q // 4, 0],
            dst_ref=crossed.at[q // 4, 1],
            send_sem=z_send.at[q // 4],
            recv_sem=z_recv.at[q // 4],
            device_id=(w, (n + 4) % 8),
            device_id_type=MESH,
        )

    def result_copy(block, q, which, send_sem, d):
        ref = rg.at[block] if which is None else rg.at[block, pl.ds(which * HALF, HALF)]
        return pltpu.make_async_remote_copy(
            src_ref=ref,
            dst_ref=ref,
            send_sem=send_sem,
            recv_sem=b_recv.at[q, which or 0],
            device_id=(w, line + (y + d) % 4),
            device_id_type=MESH,
        )

    def first_of(event):
        return place.at(table(event, [e[0] for e in EVENTS]), table(event, [e[1] for e in EVENTS]), 0)

    def square(value):
        value = value.astype(jnp.float32)
        return (value * value).astype(jnp.bfloat16)

    def add_products(event):
        first = first_of(event)
        tiles = []
        for k in range(2):
            tile = lax.dot_general(rg[first + k], ra[first + k], NT, preferred_element_type=jnp.float32)
            tiles.append(tile.reshape(COLS // (8 * WIDE), WIDE, 1, 8, ROWS))
        both = jnp.concatenate(tiles, axis=2).astype(jnp.bfloat16).reshape(COLS // (8 * WIDE), WIDE, 16, ROWS)
        for g in range(WIDE):
            products[:, pl.ds(pl.multiple_of(first * 8, 16), 16), g * ROWS : (g + 1) * ROWS] = both[:, g]

    def line_copy(source, d):
        return pltpu.make_async_remote_copy(
            src_ref=weight_line.at[source],
            dst_ref=weight_line.at[source],
            send_sem=l_send.at[d],
            recv_sem=l_recv.at[d],
            device_id=(w, line + (y + d) % 4),
            device_id_type=MESH,
        )

    def weight_copy(event, core):
        dx, dz = EVENTS[event]
        return pltpu.make_async_remote_copy(
            src_ref=weight_own,
            dst_ref=weight.at[event // 2],
            send_sem=w_send.at[event // 2, core],
            recv_sem=w_recv.at[event // 2],
            device_id=(place.at(-dx, -dz, core), n),
            device_id_type=MESH,
        )

    def hand_out(act):
        for event in range(STEPS):
            for core in range(2):
                gives = (y % 2 == c) & (y // 2 == event % 2)
                if event == 0:
                    gives = gives & (core != c)
                pl.when(gives)(functools.partial(act, event, core))

    def weight_slots(act):
        for slot in range(8):
            if slot == 0:
                pl.when((y // 2 == 1) | (y % 2 != c))(functools.partial(act, slot))
            else:
                act(slot)

    def use(event, carry):
        first = first_of(event)
        for h in range(2):
            q = 2 * event + h

            @pl.when(q % 4 == (y + 2) % 4)
            def _():
                for which in range(2):
                    result_copy(first + h, q, which, f_send.at[q], 1).wait_recv()

        r_relay.wait_other(event)
        sa = jnp.concatenate([square(ra[first + k]) for k in range(2)], axis=1)
        sg = jnp.concatenate([square(rg[first + k]) for k in range(2)], axis=1)
        corr[...] += lax.dot_general(sg, sa, NT, preferred_element_type=jnp.float32)

        add_products(event)
        return carry

    def one_step(step, carry):
        def relay():
            for event in range(1, STEPS):
                pl.when(step == event)(functools.partial(g_relay.step, event))

        if ORDER == 0:
            relay()

        @pl.when((step >= 1) & (step <= STEPS))
        def _():
            event = step - 1
            first = g_relay.wait_other(event)
            both = grads[pl.ds(first, 2)].reshape(2 * BLOCK, grads.shape[2])
            product = lax.dot_general(basis_t[...], both, NT, preferred_element_type=jnp.float32)
            for h in range(2):
                q = 2 * event + h
                parts[q] = product[:, h * BLOCK : (h + 1) * BLOCK].astype(jnp.bfloat16)

                @pl.when(q % 4 != y)
                def _():
                    share_copy(q, y, q % 4).start()

        if ORDER == 1:
            relay()

        @pl.when((step >= SUM_LAG) & (step < STEPS + SUM_LAG))
        def _():
            event = step - SUM_LAG
            for h in range(2):
                q = 2 * event + h

                @pl.when(q % 4 == y)
                def _():
                    for d in range(1, 4):
                        share_copy(q, (y + d) % 4, (y + d) % 4).wait_recv()
                    crossed[q // 4, 0] = line_sum(q).astype(jnp.bfloat16)
                    cross_copy(q).start()

        @pl.when((step >= RESULT_LAG) & (step < STEPS + RESULT_LAG))
        def _():
            event = step - RESULT_LAG
            for h in range(2):
                q = 2 * event + h

                @pl.when(q % 4 == y)
                def _():
                    cross_copy(q).wait_recv()
                    block = first_of(event) + h
                    total = (line_sum(q) + crossed[q // 4, 1].astype(jnp.float32)).astype(jnp.bfloat16)
                    rg[block] = total
                    energy[q // 4] = jnp.sum(square(total).astype(jnp.float32).reshape(COLS // 8, 8, BLOCK), axis=0)
                    result_copy(block, q, None, b_send.at[q // 4, 0], 1).start()
                    result_copy(block, q, None, b_send.at[q // 4, 1], 3).start()

        @pl.when((step >= PASS_LAG) & (step < STEPS + PASS_LAG))
        def _():
            event = step - PASS_LAG
            for h in range(2):
                q = 2 * event + h
                block = first_of(event) + h

                @pl.when(q % 4 == (y + 3) % 4)
                def _():
                    result_copy(block, q, None, f_send.at[q], 1).wait_recv()
                    result_copy(block, q, 0, f_send.at[q], 1).start()

                @pl.when(q % 4 == (y + 1) % 4)
                def _():
                    result_copy(block, q, None, f_send.at[q], 3).wait_recv()
                    result_copy(block, q, 1, f_send.at[q], 3).start()

        @pl.when(step == R_STEPS[0])
        def _():
            fetch[3].wait()
            for d in range(1, 8):
                acts_copy(d, (n + 8 - d) % 8).wait_recv()
            turned = jnp.dot(acts[...], basis_a[...], preferred_element_type=jnp.float32)
            own = turned.T.astype(jnp.bfloat16)
            ra[w] = own
            own = jnp.sum(square(own).astype(jnp.float32).reshape(ROWS // 8, 8, BLOCK), axis=0)
            weight_line[y] = jnp.broadcast_to(jnp.sum(own, axis=0, keepdims=True), (8, BLOCK))
            for d in range(1, 4):
                line_copy(y, d).start()

        for event in range(STEPS):
            pl.when(step == (R_STEPS[event]))(functools.partial(r_relay.step, event))

        @pl.when(step == ENERGY_STEP)
        def _():
            for d in range(1, 4):
                line_copy((y + 4 - d) % 4, d).wait_recv()
            weight_own[...] = weight_line[0] + weight_line[1] + weight_line[2] + weight_line[3]
            hand_out(lambda event, core: weight_copy(event, core).start())

            @pl.when((y // 2 == 0) & (y % 2 == c))
            def _():
                weight[0] = weight_own[...]

        @pl.when(step == STEPS + RESULT_LAG - 1)
        def _():
            weight_slots(lambda slot: weight_copy(2 * slot, 0).wait_recv())
            total = jnp.zeros((8, BLOCK), jnp.float32)
            for slot in range(8):
                total = total + weight[slot] * energy[slot]
            total = jnp.full((8, 128), jnp.sum(total), jnp.float32)
            sum_begin(0, total, small.at[0], send_s.at[0], recv_s.at[0])

        @pl.when(step == STEPS + RESULT_LAG + 1)
        def _():
            total = sum_end(0, small.at[0], send_s.at[0], recv_s.at[0])
            sum_begin(1, total, small.at[1], send_s.at[1], recv_s.at[1])

        @pl.when(step >= USE_STEP)
        def _():
            lax.fori_loop(2 * (step - USE_STEP), 2 * (step - USE_STEP) + 2, use, 0)

        return carry

    lax.fori_loop(1, USE_STEP + STEPS // 2, one_step, 0)
    moments = corr[...] * (1.0 / TOKENS)
    corr[...] = moments
    total = sum_end(1, small.at[1], send_s.at[1], recv_s.at[1])
    damping = (0.1 / (float(D) * FF * TOKENS)) * total[0:1, 0:1]
    flipped = (1.0 / (moments + damping)).reshape(COLS // (8 * WIDE), WIDE, 8, ROWS)
    for g in range(WIDE):
        recip[:, :, g * ROWS : (g + 1) * ROWS] = flipped[:, g]

    def add_gram(group, carry):
        tile = products[group]
        scaled = (tile.astype(jnp.float32).reshape(NB, 8, WIDE * ROWS) * recip[group][None]).astype(jnp.bfloat16)
        gram[...] += lax.dot_general(
            scaled.reshape(NB * 8, WIDE * ROWS), tile, NT, preferred_element_type=jnp.float32
        )
        return carry

    lax.fori_loop(0, COLS // (8 * WIDE), add_gram, 0)
    size = NB * 8
    rows = lax.broadcasted_iota(jnp.int32, (size, size), 0) % 8
    cols = lax.broadcasted_iota(jnp.int32, (size, size), 1) % 8
    own = jnp.where(rows == cols, gram[...], 0.0).reshape(NB, 8, size)
    own = jnp.sum(own, axis=1)
    pick = lax.broadcasted_iota(jnp.int32, (size, 128), 0) // 8 == lax.broadcasted_iota(jnp.int32, (size, 128), 1)
    exact = dict(precision=lax.Precision.HIGHEST, preferred_element_type=jnp.float32)
    kernel_t = jnp.dot(own, pick.astype(jnp.float32), **exact)
    packed = jnp.concatenate([kernel_t[8 * k : 8 * k + 8, :NB] for k in range(4)], axis=1)
    for stage in range(2):
        sum_begin(stage, packed, large.at[stage], send_l.at[stage], recv_l.at[stage])
        packed = sum_end(stage, large.at[stage], send_l.at[stage], recv_l.at[stage])
    kernel_t = jnp.concatenate([packed[:, NB * k : NB * k + NB] for k in range(4)], axis=0)

    pairs = probe_ref.shape[1]
    ids = lax.broadcasted_iota(jnp.int32, (NB, pairs), 0)
    pick_c = (probe_ref[0:1, :] == ids).astype(jnp.float32)
    pick_r = (probe_ref[1:2, :] == ids).astype(jnp.float32)
    spread = jnp.dot(kernel_t, pick_c - pick_r, **exact)
    keep = 1.0 - pick_c - pick_r
    owner = (source_ref[...] == lax.broadcasted_iota(jnp.int32, (SOURCES, NB), 0)).astype(jnp.float32)
    factor = 1.0 / (BLOCK * math.sqrt(D * FF))
    influence[...] = jnp.dot(owner, spread * keep, **exact) * factor

    for i in range(8):
        for d in range(1, 4):
            share_copy(4 * i + (y + d) % 4, y, (y + d) % 4).wait_send()
        cross_copy(4 * i).wait_send()
        result_copy(0, 0, None, b_send.at[i, 0], 1).wait_send()
        result_copy(0, 0, None, b_send.at[i, 1], 3).wait_send()
        result_copy(0, 0, 0, f_send.at[4 * i + (y + 3) % 4], 1).wait_send()
        result_copy(0, 0, 1, f_send.at[4 * i + (y + 1) % 4], 3).wait_send()
    for d in range(1, 8):
        acts_copy(d, n).wait_send()
    for d in range(1, 4):
        line_copy(y, d).wait_send()
    hand_out(lambda event, core: weight_copy(event, core).wait_send())
    g_relay.finish()
    r_relay.finish()


def whole_call(acts, grads, basis_a, basis_t, source, probe):
    anywhere = pl.BlockSpec(memory_space=pl.ANY)
    whole = pl.BlockSpec(memory_space=pltpu.VMEM)
    dma = pltpu.SemaphoreType.DMA
    bf16, f32 = jnp.bfloat16, jnp.float32
    hidden = grads.shape[1]
    return pl.pallas_call(
        whole_kernel,
        out_shape=(
            jax.ShapeDtypeStruct((COLS, ROWS), f32),
            jax.ShapeDtypeStruct((SOURCES, probe.shape[1]), f32),
        ),
        in_specs=[anywhere] * 4 + [whole] * 2,
        out_specs=(whole, whole),
        scratch_shapes=[
            pltpu.VMEM((NB, BLOCK, hidden), bf16),
            pltpu.VMEM((BLOCK, D), bf16),
            pltpu.VMEM((D, ROWS), bf16),
            pltpu.VMEM((COLS, hidden), bf16),
            pltpu.VMEM((NB, COLS, BLOCK), bf16),
            pltpu.VMEM((8, 4, COLS, BLOCK), bf16),
            pltpu.VMEM((8, 2, COLS, BLOCK), bf16),
            pltpu.VMEM((NB, ROWS, BLOCK), bf16),
            pltpu.VMEM((NB, COLS, BLOCK), bf16),
            pltpu.VMEM((COLS // (8 * WIDE), NB * 8, WIDE * ROWS), bf16),
            pltpu.VMEM((NB * 8, NB * 8), f32),
            pltpu.VMEM((COLS // (8 * WIDE), 8, WIDE * ROWS), f32),
            pltpu.VMEM((2, 16, 8, 128), f32),
            pltpu.VMEM((2, 16, 8, 128), f32),
            pltpu.VMEM((8, 8, 128), f32),
            pltpu.VMEM((8, 8, 128), f32),
            pltpu.VMEM((4, 8, 128), f32),
            pltpu.VMEM((8, 128), f32),
            dma((4,)),
            dma((STEPS, 5)),
            dma((STEPS, 2)),
            dma((STEPS,)),
            dma((STEPS, 5)),
            dma((STEPS, 2)),
            dma((STEPS,)),
            dma((8,)),
            dma((8,)),
            dma((NB,)),
            dma((8, 4)),
            dma((8,)),
            dma((8,)),
            dma((8, 2)),
            dma((NB, 2)),
            dma((NB,)),
            dma((2,)),
            dma((2,)),
            dma((2,)),
            dma((2,)),
            dma((4,)),
            dma((4,)),
            dma((8, 2)),
            dma((8,)),
        ],
        compiler_params=pltpu.CompilerParams(
            collective_id=1, has_side_effects=True, vmem_limit_bytes=60 * 1024 * 1024
        ),
        cost_estimate=pl.CostEstimate(flops=10**10, bytes_accessed=10**7, transcendentals=0),
    )(acts, grads, basis_a, basis_t, source, probe)


def on_device(acts, grads, basis_a, basis_g, source_of_block, probe_blocks):
    correction, influence = whole_call(
        acts, grads, basis_a, basis_g.T, source_of_block.T, probe_blocks.T
    )
    return (correction.T, influence.T)


def solution(mesh):
    placed = (
        P("wide", "narrow"),
        P("wide", "narrow"),
        P(None, "narrow"),
        P("narrow", "wide"),
        P(),
        P(),
    )
    return jax.shard_map(
        on_device, mesh=mesh, in_specs=placed, out_specs=(P("narrow", "wide"), P()), check_vma=False
    )
```

```python
import functools
import math

import jax
import jax.numpy as jnp
from jax import lax
from jax.experimental import pallas as pl
from jax.experimental.pallas import tpu as pltpu
from jax.sharding import PartitionSpec as P

D = 4096
FF = 14336
BLOCK = 128
SOURCES = 16
NB = 32
TOKENS = 4096
ROWS = D // 8
COLS = FF // 32
MESH = pl.DeviceIdType.MESH
NT = (((1,), (1,)), ((), ()))
STAGES = (16, 16)


def stage_peers():
    w, n = lax.axis_index("wide"), lax.axis_index("narrow")
    near, far = (w % 2) * 8 + n, w // 2

    def peer(stage, d):
        if stage == 0:
            other = (near + d) % 16
            return (far * 2 + other // 8, other % 8)
        return (((far + d) % 16) * 2 + w % 2, n)

    return peer, (near, far)


def sum_copy(stage, slots, send, recv, source, d):
    peer, _ = stage_peers()
    return pltpu.make_async_remote_copy(
        src_ref=slots.at[source],
        dst_ref=slots.at[source],
        send_sem=send,
        recv_sem=recv,
        device_id=peer(stage, d),
        device_id_type=MESH,
    )


def sum_begin(stage, value, slots, send, recv):
    mine = stage_peers()[1][stage]
    slots[mine] = value
    for d in range(1, STAGES[stage]):
        sum_copy(stage, slots, send, recv, mine, d).start()


def sum_end(stage, slots, send, recv):
    size = STAGES[stage]
    sum_copy(stage, slots, send, recv, pl.ds(0, size - 1), 1).wait()
    total = slots[0]
    for s in range(1, size):
        total = total + slots[s]
    return total


EVENTS = (
    (0, 0), (-1, 0), (1, 0), (0, -1), (0, 1), (2, 0), (0, 2), (-1, -1),
    (1, -1), (-1, 1), (1, 1), (2, -1), (2, 1), (-1, 2), (1, 2), (2, 2),
)
STEPS = len(EVENTS)
R_STEPS = (10, 13, 14, 15, 15, 16, 16, 17, 18, 19, 19, 20, 21, 22, 22, 23)
ORDER = 1
ENERGY_STEP = 12
SUM_LAG = 3
RESULT_LAG = 6
PASS_LAG = 8
USE_STEP = 17
HALF = COLS // 2
WIDE = 7


def table(step, values):
    picked = jnp.int32(values[0])
    for index, value in enumerate(values):
        if index:
            picked = jnp.where(step == index, jnp.int32(value), picked)
    return picked


class Place:
    def __init__(self):
        self.w, self.n = lax.axis_index("wide"), lax.axis_index("narrow")
        self.x, self.z, self.c = self.w // 8, (self.w // 2) % 4, self.w % 2

    def at(self, dx, dz, c):
        return ((self.x + dx + 4) % 4) * 8 + ((self.z + dz + 4) % 4) * 2 + c

    def owned(self, event, c):
        return self.at(*EVENTS[event], c)


class Relay:
    def __init__(self, place, buffer, send, recv, other):
        self.place, self.buffer, self.send, self.recv, self.other = place, buffer, send, recv, other
        self.half = buffer.shape[1] // 2

    def part(self, chunk, which):
        if which is None:
            return self.buffer.at[chunk]
        return self.buffer.at[chunk, pl.ds(which * self.half, self.half)]

    def copy(self, event, which, slot, recv_sem, dx, dz, dc=0):
        place = self.place
        ref = self.part(place.owned(event, place.c), which)
        c = (place.c + dc) % 2
        return pltpu.make_async_remote_copy(
            src_ref=ref,
            dst_ref=ref,
            send_sem=self.send.at[event, slot],
            recv_sem=recv_sem,
            device_id=(place.at(dx, dz, c), place.n),
            device_id_type=MESH,
        )

    def sends(self, event):
        dx, dz = EVENTS[event]
        recv = self.recv
        found = []
        if dx == 0:
            found.append(self.copy(event, None, 1, recv.at[EVENTS.index((-1, dz)), 0], 1, 0))
            found.append(self.copy(event, None, 2, recv.at[EVENTS.index((1, dz)), 0], -1, 0))
        if (dx, dz) == (0, 0):
            found.append(self.copy(event, None, 3, recv.at[EVENTS.index((0, -1)), 0], 0, 1))
            found.append(self.copy(event, None, 4, recv.at[EVENTS.index((0, 1)), 0], 0, -1))
        if (dx, dz) == (0, -1):
            found.append(self.copy(event, 0, 3, recv.at[EVENTS.index((0, 2)), 0], 0, 1))
        if (dx, dz) == (0, 1):
            found.append(self.copy(event, 1, 4, recv.at[EVENTS.index((0, 2)), 1], 0, -1))
        if dx == -1:
            found.append(self.copy(event, 0, 1, recv.at[EVENTS.index((2, dz)), 0], 1, 0))
        if dx == 1:
            found.append(self.copy(event, 1, 2, recv.at[EVENTS.index((2, dz)), 1], -1, 0))
        found.append(self.copy(event, None, 0, self.other.at[event], 0, 0, 1))
        return found

    def wait_arrival(self, event):
        dx, dz = EVENTS[event]
        if (dx, dz) == (0, 0):
            return
        halves = (0, 1) if dx == 2 or dz == 2 and dx == 0 else (None,)
        for which in halves:
            self.copy(event, which, 0, self.recv.at[event, which or 0], 0, 0, 1).wait_recv()

    def step(self, event):
        self.wait_arrival(event)
        for copy in self.sends(event):
            copy.start()

    def wait_other(self, event):
        place = self.place
        dx = table(event, [e[0] for e in EVENTS])
        dz = table(event, [e[1] for e in EVENTS])
        ref = self.buffer.at[place.at(dx, dz, 1 - place.c)]
        pltpu.make_async_remote_copy(
            src_ref=ref,
            dst_ref=ref,
            send_sem=self.send.at[0, 0],
            recv_sem=self.other.at[event],
            device_id=(place.at(0, 0, 1 - place.c), place.n),
            device_id_type=MESH,
        ).wait_recv()
        return place.at(dx, dz, 0)

    def finish(self):
        for event in range(STEPS):
            for copy in self.sends(event):
                copy.wait_send()


def whole_kernel(
    acts_hbm, grads_hbm, basis_a_hbm, basis_t_hbm, source_ref, probe_ref, corr, influence,
    grads, acts, basis_a, basis_t, parts, shares, crossed, ra, rg, products, gram, recip, small, large,
    energy, weight, weight_line, weight_own,
    local, g_send, g_recv, g_other, r_send, r_recv, r_other,
    a_send, a_recv, s_send, s_recv, z_send, z_recv, b_send, b_recv, f_send, send_s, recv_s, send_l, recv_l,
    l_send, l_recv, w_send, w_recv,
):
    place = Place()
    w, n, c = place.w, place.n, place.c
    y, line = n % 4, (n // 4) * 4
    width = acts_hbm.shape[1]
    own_cols = pl.ds(pl.multiple_of(n * width, width), width)
    fetch = [
        pltpu.make_async_copy(grads_hbm, grads.at[w], local.at[0]),
        pltpu.make_async_copy(acts_hbm, acts.at[:, own_cols], local.at[1]),
        pltpu.make_async_copy(basis_t_hbm, basis_t, local.at[2]),
        pltpu.make_async_copy(basis_a_hbm, basis_a, local.at[3]),
    ]
    for copy in fetch:
        copy.start()
    peer, _ = stage_peers()
    barrier = pltpu.get_barrier_semaphore()
    count = 0
    for stage, size in enumerate(STAGES):
        for d in range(1, size):
            pl.semaphore_signal(barrier, inc=1, device_id=peer(stage, d), device_id_type=MESH)
            count += 1
    for event in range(1, STEPS):
        dx, dz = EVENTS[event]
        pl.semaphore_signal(barrier, inc=1, device_id=(place.at(dx, dz, 1 - c), n), device_id_type=MESH)
        count += 1
    pl.semaphore_wait(barrier, count)

    g_relay = Relay(place, grads, g_send, g_recv, g_other)
    r_relay = Relay(place, ra, r_send, r_recv, r_other)
    fetch[0].wait()
    g_relay.step(0)

    def acts_copy(d, source):
        cols = pl.ds(pl.multiple_of(source * width, width), width)
        return pltpu.make_async_remote_copy(
            src_ref=acts.at[:, cols],
            dst_ref=acts.at[:, cols],
            send_sem=a_send.at[d],
            recv_sem=a_recv.at[d],
            device_id=(w, (n + d) % 8),
            device_id_type=MESH,
        )

    fetch[1].wait()
    for d in range(1, 8):
        acts_copy(d, n).start()
    corr[...] = jnp.zeros_like(corr)
    gram[...] = jnp.zeros_like(gram)
    fetch[2].wait()

    def share_copy(q, source, target):
        return pltpu.make_async_remote_copy(
            src_ref=parts.at[q],
            dst_ref=shares.at[q // 4, source],
            send_sem=s_send.at[q],
            recv_sem=s_recv.at[q // 4, source],
            device_id=(w, line + target),
            device_id_type=MESH,
        )

    def line_sum(q):
        total = parts[q].astype(jnp.float32)
        for d in range(1, 4):
            total = total + shares[q // 4, (y + d) % 4].astype(jnp.float32)
        return total

    def cross_copy(q):
        return pltpu.make_async_remote_copy(
            src_ref=crossed.at[q // 4, 0],
            dst_ref=crossed.at[q // 4, 1],
            send_sem=z_send.at[q // 4],
            recv_sem=z_recv.at[q // 4],
            device_id=(w, (n + 4) % 8),
            device_id_type=MESH,
        )

    def result_copy(block, q, which, send_sem, d):
        ref = rg.at[block] if which is None else rg.at[block, pl.ds(which * HALF, HALF)]
        return pltpu.make_async_remote_copy(
            src_ref=ref,
            dst_ref=ref,
            send_sem=send_sem,
            recv_sem=b_recv.at[q, which or 0],
            device_id=(w, line + (y + d) % 4),
            device_id_type=MESH,
        )

    def first_of(event):
        return place.at(table(event, [e[0] for e in EVENTS]), table(event, [e[1] for e in EVENTS]), 0)

    def square(value):
        value = value.astype(jnp.float32)
        return (value * value).astype(jnp.bfloat16)

    def add_products(event):
        first = first_of(event)
        tiles = []
        for k in range(2):
            tile = lax.dot_general(rg[first + k], ra[first + k], NT, preferred_element_type=jnp.float32)
            tiles.append(tile.reshape(COLS // (8 * WIDE), WIDE, 1, 8, ROWS))
        both = jnp.concatenate(tiles, axis=2).astype(jnp.bfloat16).reshape(COLS // (8 * WIDE), WIDE, 16, ROWS)
        for g in range(WIDE):
            products[:, pl.ds(pl.multiple_of(first * 8, 16), 16), g * ROWS : (g + 1) * ROWS] = both[:, g]

    def line_copy(source, d):
        return pltpu.make_async_remote_copy(
            src_ref=weight_line.at[source],
            dst_ref=weight_line.at[source],
            send_sem=l_send.at[d],
            recv_sem=l_recv.at[d],
            device_id=(w, line + (y + d) % 4),
            device_id_type=MESH,
        )

    def weight_copy(event, core):
        dx, dz = EVENTS[event]
        return pltpu.make_async_remote_copy(
            src_ref=weight_own,
            dst_ref=weight.at[event // 2],
            send_sem=w_send.at[event // 2, core],
            recv_sem=w_recv.at[event // 2],
            device_id=(place.at(-dx, -dz, core), n),
            device_id_type=MESH,
        )

    def hand_out(act):
        for event in range(STEPS):
            for core in range(2):
                gives = (y % 2 == c) & (y // 2 == event % 2)
                if event == 0:
                    gives = gives & (core != c)
                pl.when(gives)(functools.partial(act, event, core))

    def weight_slots(act):
        for slot in range(8):
            if slot == 0:
                pl.when((y // 2 == 1) | (y % 2 != c))(functools.partial(act, slot))
            else:
                act(slot)

    def use(event, carry):
        first = first_of(event)
        for h in range(2):
            q = 2 * event + h

            @pl.when(q % 4 == (y + 2) % 4)
            def _():
                for which in range(2):
                    result_copy(first + h, q, which, f_send.at[q], 1).wait_recv()

        r_relay.wait_other(event)
        sa = jnp.concatenate([square(ra[first + k]) for k in range(2)], axis=1)
        sg = jnp.concatenate([square(rg[first + k]) for k in range(2)], axis=1)
        corr[...] += lax.dot_general(sg, sa, NT, preferred_element_type=jnp.float32)

        add_products(event)
        return carry

    def one_step(step, carry):
        def relay():
            for event in range(1, STEPS):
                pl.when(step == event)(functools.partial(g_relay.step, event))

        if ORDER == 0:
            relay()

        @pl.when((step >= 1) & (step <= STEPS))
        def _():
            event = step - 1
            first = g_relay.wait_other(event)
            both = grads[pl.ds(first, 2)].reshape(2 * BLOCK, grads.shape[2])
            product = lax.dot_general(basis_t[...], both, NT, preferred_element_type=jnp.float32)
            for h in range(2):
                q = 2 * event + h
                parts[q] = product[:, h * BLOCK : (h + 1) * BLOCK].astype(jnp.bfloat16)

                @pl.when(q % 4 != y)
                def _():
                    share_copy(q, y, q % 4).start()

        if ORDER == 1:
            relay()

        @pl.when((step >= SUM_LAG) & (step < STEPS + SUM_LAG))
        def _():
            event = step - SUM_LAG
            for h in range(2):
                q = 2 * event + h

                @pl.when(q % 4 == y)
                def _():
                    for d in range(1, 4):
                        share_copy(q, (y + d) % 4, (y + d) % 4).wait_recv()
                    crossed[q // 4, 0] = line_sum(q).astype(jnp.bfloat16)
                    cross_copy(q).start()

        @pl.when((step >= RESULT_LAG) & (step < STEPS + RESULT_LAG))
        def _():
            event = step - RESULT_LAG
            for h in range(2):
                q = 2 * event + h

                @pl.when(q % 4 == y)
                def _():
                    cross_copy(q).wait_recv()
                    block = first_of(event) + h
                    total = (line_sum(q) + crossed[q // 4, 1].astype(jnp.float32)).astype(jnp.bfloat16)
                    rg[block] = total
                    energy[q // 4] = jnp.sum(square(total).astype(jnp.float32).reshape(COLS // 8, 8, BLOCK), axis=0)
                    result_copy(block, q, None, b_send.at[q // 4, 0], 1).start()
                    result_copy(block, q, None, b_send.at[q // 4, 1], 3).start()

        @pl.when((step >= PASS_LAG) & (step < STEPS + PASS_LAG))
        def _():
            event = step - PASS_LAG
            for h in range(2):
                q = 2 * event + h
                block = first_of(event) + h

                @pl.when(q % 4 == (y + 3) % 4)
                def _():
                    result_copy(block, q, None, f_send.at[q], 1).wait_recv()
                    result_copy(block, q, 0, f_send.at[q], 1).start()

                @pl.when(q % 4 == (y + 1) % 4)
                def _():
                    result_copy(block, q, None, f_send.at[q], 3).wait_recv()
                    result_copy(block, q, 1, f_send.at[q], 3).start()

        @pl.when(step == R_STEPS[0])
        def _():
            fetch[3].wait()
            for d in range(1, 8):
                acts_copy(d, (n + 8 - d) % 8).wait_recv()
            turned = jnp.dot(acts[...], basis_a[...], preferred_element_type=jnp.float32)
            own = turned.T.astype(jnp.bfloat16)
            ra[w] = own
            own = jnp.sum(square(own).astype(jnp.float32).reshape(ROWS // 8, 8, BLOCK), axis=0)
            weight_line[y] = jnp.broadcast_to(jnp.sum(own, axis=0, keepdims=True), (8, BLOCK))
            for d in range(1, 4):
                line_copy(y, d).start()

        for event in range(STEPS):
            pl.when(step == (R_STEPS[event]))(functools.partial(r_relay.step, event))

        @pl.when(step == ENERGY_STEP)
        def _():
            for d in range(1, 4):
                line_copy((y + 4 - d) % 4, d).wait_recv()
            weight_own[...] = weight_line[0] + weight_line[1] + weight_line[2] + weight_line[3]
            hand_out(lambda event, core: weight_copy(event, core).start())

            @pl.when((y // 2 == 0) & (y % 2 == c))
            def _():
                weight[0] = weight_own[...]

        @pl.when(step == STEPS + RESULT_LAG - 1)
        def _():
            weight_slots(lambda slot: weight_copy(2 * slot, 0).wait_recv())
            total = jnp.zeros((8, BLOCK), jnp.float32)
            for slot in range(8):
                total = total + weight[slot] * energy[slot]
            total = jnp.full((8, 128), jnp.sum(total), jnp.float32)
            sum_begin(0, total, small.at[0], send_s.at[0], recv_s.at[0])

        @pl.when(step == STEPS + RESULT_LAG + 1)
        def _():
            total = sum_end(0, small.at[0], send_s.at[0], recv_s.at[0])
            sum_begin(1, total, small.at[1], send_s.at[1], recv_s.at[1])

        @pl.when(step >= USE_STEP)
        def _():
            lax.fori_loop(2 * (step - USE_STEP), 2 * (step - USE_STEP) + 2, use, 0)

        return carry

    lax.fori_loop(1, USE_STEP + STEPS // 2, one_step, 0)
    moments = corr[...] * (1.0 / TOKENS)
    corr[...] = moments
    total = sum_end(1, small.at[1], send_s.at[1], recv_s.at[1])
    damping = (0.1 / (float(D) * FF * TOKENS)) * total[0:1, 0:1]
    flipped = (1.0 / (moments + damping)).reshape(COLS // (8 * WIDE), WIDE, 8, ROWS)
    for g in range(WIDE):
        recip[:, :, g * ROWS : (g + 1) * ROWS] = flipped[:, g]

    def add_gram(group, carry):
        tile = products[group]
        scaled = (tile.astype(jnp.float32).reshape(NB, 8, WIDE * ROWS) * recip[group][None]).astype(jnp.bfloat16)
        gram[...] += lax.dot_general(
            scaled.reshape(NB * 8, WIDE * ROWS), tile, NT, preferred_element_type=jnp.float32
        )
        return carry

    lax.fori_loop(0, COLS // (8 * WIDE), add_gram, 0)
    size = NB * 8
    rows = lax.broadcasted_iota(jnp.int32, (size, size), 0) % 8
    cols = lax.broadcasted_iota(jnp.int32, (size, size), 1) % 8
    own = jnp.where(rows == cols, gram[...], 0.0).reshape(NB, 8, size)
    own = jnp.sum(own, axis=1)
    pick = lax.broadcasted_iota(jnp.int32, (size, 128), 0) // 8 == lax.broadcasted_iota(jnp.int32, (size, 128), 1)
    exact = dict(precision=lax.Precision.HIGHEST, preferred_element_type=jnp.float32)
    kernel_t = jnp.dot(own, pick.astype(jnp.float32), **exact)
    packed = jnp.concatenate([kernel_t[8 * k : 8 * k + 8, :NB] for k in range(4)], axis=1)
    for stage in range(2):
        sum_begin(stage, packed, large.at[stage], send_l.at[stage], recv_l.at[stage])
        packed = sum_end(stage, large.at[stage], send_l.at[stage], recv_l.at[stage])
    kernel_t = jnp.concatenate([packed[:, NB * k : NB * k + NB] for k in range(4)], axis=0)

    pairs = probe_ref.shape[1]
    ids = lax.broadcasted_iota(jnp.int32, (NB, pairs), 0)
    pick_c = (probe_ref[0:1, :] == ids).astype(jnp.float32)
    pick_r = (probe_ref[1:2, :] == ids).astype(jnp.float32)
    spread = jnp.dot(kernel_t, pick_c - pick_r, **exact)
    keep = 1.0 - pick_c - pick_r
    owner = (source_ref[...] == lax.broadcasted_iota(jnp.int32, (SOURCES, NB), 0)).astype(jnp.float32)
    factor = 1.0 / (BLOCK * math.sqrt(D * FF))
    influence[...] = jnp.dot(owner, spread * keep, **exact) * factor

    for i in range(8):
        for d in range(1, 4):
            share_copy(4 * i + (y + d) % 4, y, (y + d) % 4).wait_send()
        cross_copy(4 * i).wait_send()
        result_copy(0, 0, None, b_send.at[i, 0], 1).wait_send()
        result_copy(0, 0, None, b_send.at[i, 1], 3).wait_send()
        result_copy(0, 0, 0, f_send.at[4 * i + (y + 3) % 4], 1).wait_send()
        result_copy(0, 0, 1, f_send.at[4 * i + (y + 1) % 4], 3).wait_send()
    for d in range(1, 8):
        acts_copy(d, n).wait_send()
    for d in range(1, 4):
        line_copy(y, d).wait_send()
    hand_out(lambda event, core: weight_copy(event, core).wait_send())
    g_relay.finish()
    r_relay.finish()


def whole_call(acts, grads, basis_a, basis_t, source, probe):
    anywhere = pl.BlockSpec(memory_space=pl.ANY)
    whole = pl.BlockSpec(memory_space=pltpu.VMEM)
    dma = pltpu.SemaphoreType.DMA
    bf16, f32 = jnp.bfloat16, jnp.float32
    hidden = grads.shape[1]
    return pl.pallas_call(
        whole_kernel,
        out_shape=(
            jax.ShapeDtypeStruct((COLS, ROWS), f32),
            jax.ShapeDtypeStruct((SOURCES, probe.shape[1]), f32),
        ),
        in_specs=[anywhere] * 4 + [whole] * 2,
        out_specs=(whole, whole),
        scratch_shapes=[
            pltpu.VMEM((NB, BLOCK, hidden), bf16),
            pltpu.VMEM((BLOCK, D), bf16),
            pltpu.VMEM((D, ROWS), bf16),
            pltpu.VMEM((COLS, hidden), bf16),
            pltpu.VMEM((NB, COLS, BLOCK), bf16),
            pltpu.VMEM((8, 4, COLS, BLOCK), bf16),
            pltpu.VMEM((8, 2, COLS, BLOCK), bf16),
            pltpu.VMEM((NB, ROWS, BLOCK), bf16),
            pltpu.VMEM((NB, COLS, BLOCK), bf16),
            pltpu.VMEM((COLS // (8 * WIDE), NB * 8, WIDE * ROWS), bf16),
            pltpu.VMEM((NB * 8, NB * 8), f32),
            pltpu.VMEM((COLS // (8 * WIDE), 8, WIDE * ROWS), f32),
            pltpu.VMEM((2, 16, 8, 128), f32),
            pltpu.VMEM((2, 16, 8, 128), f32),
            pltpu.VMEM((8, 8, 128), f32),
            pltpu.VMEM((8, 8, 128), f32),
            pltpu.VMEM((4, 8, 128), f32),
            pltpu.VMEM((8, 128), f32),
            dma((4,)),
            dma((STEPS, 5)),
            dma((STEPS, 2)),
            dma((STEPS,)),
            dma((STEPS, 5)),
            dma((STEPS, 2)),
            dma((STEPS,)),
            dma((8,)),
            dma((8,)),
            dma((NB,)),
            dma((8, 4)),
            dma((8,)),
            dma((8,)),
            dma((8, 2)),
            dma((NB, 2)),
            dma((NB,)),
            dma((2,)),
            dma((2,)),
            dma((2,)),
            dma((2,)),
            dma((4,)),
            dma((4,)),
            dma((8, 2)),
            dma((8,)),
        ],
        compiler_params=pltpu.CompilerParams(
            collective_id=1, has_side_effects=True, vmem_limit_bytes=60 * 1024 * 1024
        ),
        cost_estimate=pl.CostEstimate(flops=10**10, bytes_accessed=10**7, transcendentals=0),
    )(acts, grads, basis_a, basis_t, source, probe)


def on_device(acts, grads, basis_a, basis_g, source_of_block, probe_blocks):
    correction, influence = whole_call(
        acts, grads, basis_a, basis_g.T, source_of_block.T, probe_blocks.T
    )
    return (correction.T, influence.T)


def solution(mesh):
    placed = (
        P("wide", "narrow"),
        P("wide", "narrow"),
        P(None, "narrow"),
        P("narrow", "wide"),
        P(),
        P(),
    )
    return jax.shard_map(
        on_device, mesh=mesh, in_specs=placed, out_specs=(P("narrow", "wide"), P()), check_vma=False
    )
```
